32 devices in a mesh: tile: 8 (over z, x), ens: 4 (over y, core).
Axes of the slice: x: 2, y: 2, z: 4, core: 2. Of those that a mesh axis runs over, the one named last changes fastest.
Arguments:
- features: bfloat16 [4, 8, 16, 16, 256], P('ens', 'tile'), may hold values from -6 to 6
- cotangent: bfloat16 [4, 8, 16, 16, 256], P('ens', 'tile'), may hold values from -6 to 6
- kernel: float32 [49, 256], replicated, may hold values from -0.875 to 0.875
- weight_in: bfloat16 [256, 1024], replicated, may hold values from -0.375 to 0.375
- weight_out: bfloat16 [1024, 256], replicated, may hold values from -0.1875 to 0.1875
- tile_neighbour: int32 [8, 4], P('tile'), may hold values from 0 to 7, as said below
- edge_code: int32 [8, 4], P('tile'), may hold values from 0 to 7, as said below
Outputs:
- grad_features: bfloat16 [4, 8, 16, 16, 256], P('ens', 'tile')
- grad_kernel: float32 [49, 256], replicated
- grad_weight_in: float32 [256, 1024], replicated
- grad_weight_out: float32 [1024, 256], replicated
The draws below stay inside these ranges and needn't reach their ends.
Inputs may be any that keep to these rules, and one draw needn't show every extreme that they name: `tile_neighbour`: tile t is held by index t // 1 of tile; every neighbour of tile t is held by that same index, the one before it or the one after it, cyclically. edge_code % 4 names the neighbour's edge (0 top, 1 bottom, 2 left, 3 right); 4 or more means reversed along the edge.
All inputs are finite; a program needn't handle non-finite values.
Results may differ from the reference program's by a relative error of at most 0.015.
Values may be sent and summed in bfloat16 or wider, within the bound.
No kernel may reach another device: no remote copies, remote signals or barrier semaphores. Data moves between devices by JAX's collectives and lax.ppermute only.
A program may use at most 64 MiB of HBM per device.

```python
import math
import jax
import jax.numpy as jnp
from jax import lax

C = 256
HID = 1024
KERNEL_TAPS = 7
DILATION_STEP = 2
HALO = 6
TILE = 16
TPD = 1
MEMBERS = 4
TILES = 8


def draw_tile_neighbour(key, part):
    first_key, second_key = jax.random.split(jax.random.fold_in(key, 11))
    owners = TILES // TPD
    tile_ids = jnp.arange(TILES, dtype=jnp.int32)
    holder = tile_ids // TPD
    offset = jax.random.randint(first_key, (TILES, 4), -1, 2, dtype=jnp.int32)
    within = jax.random.randint(second_key, (TILES, 4), 0, TPD, dtype=jnp.int32)
    chosen = (holder[:, None] + offset) % owners * TPD + within
    chosen = chosen.at[0, 0].set(TILES - 1)
    chosen = chosen.at[0, 1].set(0)
    return chosen.astype(jnp.int32)


def draw_edge_code(key, part):
    codes = jax.random.randint(jax.random.fold_in(key, 23), (TILES, 4), 0, 8, dtype=jnp.int32)
    codes = codes.at[0, 2].set(7)
    codes = codes.at[0, 3].set(0)
    return codes.astype(jnp.int32)


def shard_levels(own_key, extent, pieces, least, top_value):
    level, own = 1.0, jax.random.fold_in(own_key, 6)
    for dim, shards_of in pieces:
        steps = jnp.exp(jax.random.uniform(jax.random.fold_in(own, dim), (shards_of,), jnp.float32, least / len(pieces), top_value / len(pieces)))
        level = level * jnp.repeat(steps, extent[dim] // shards_of).reshape([-1 if axis == dim else 1 for axis in range(len(extent))])
    return level


def gaussian(key, dims, spread, reach, pieces=(), kind=jnp.bfloat16):
    array = jax.random.normal(key, dims, jnp.float32) * spread
    if len(pieces) > 0:
        array = shard_levels(key, dims, pieces, -0.22, 0.18) * array
    return jnp.clip(array, min=-reach, max=reach).astype(kind)


def setup_inputs(seed: int = 0) -> dict:
    splits = jax.random.split(jax.random.key(seed), 8)
    features = gaussian(splits[0], (MEMBERS, TILES, TILE, TILE, C), 1.0, 6.0, ((0, 4), (1, 8)))
    cotangent = gaussian(splits[1], (MEMBERS, TILES, TILE, TILE, C), 1.0, 6.0, ((0, 4), (1, 8)))
    kernel = gaussian(splits[2], (KERNEL_TAPS * KERNEL_TAPS, C), (KERNEL_TAPS * KERNEL_TAPS) ** -0.5, 0.875, (), jnp.float32)
    weight_in = gaussian(splits[3], (C, HID), C ** -0.5, 0.375)
    weight_out = gaussian(splits[4], (HID, C), HID ** -0.5, 0.1875)
    tile_neighbour = draw_tile_neighbour(jax.random.fold_in(splits[7], 71), 0)
    edge_code = draw_edge_code(jax.random.fold_in(splits[7], 71), 0)
    return dict(features=features, cotangent=cotangent, kernel=kernel, weight_in=weight_in, weight_out=weight_out, tile_neighbour=tile_neighbour, edge_code=edge_code)


def pad_axis(values, from_end, before, later):
    widths = [(0, 0)] * values.ndim
    widths[values.ndim - from_end] = (before, later)
    return jnp.pad(values, widths)

def edge_strips(field_in, depth_rows):
    top_side = field_in[..., :depth_rows, :, :]
    bottom_side = jnp.flip(field_in[..., -depth_rows:, :, :], -3)
    left_side = jnp.swapaxes(field_in[..., :, :depth_rows, :], -3, -2)
    right_side = jnp.swapaxes(jnp.flip(field_in[..., :, -depth_rows:, :], -2), -3, -2)
    return jnp.stack([top_side, bottom_side, left_side, right_side], -4)

def place_edges(strips, edge_length):
    depth_rows = strips.shape[-3]
    extra = edge_length - depth_rows
    top_side = pad_axis(strips[..., 0, :, :, :], 3, 0, extra)
    bottom_side = pad_axis(jnp.flip(strips[..., 1, :, :, :], -3), 3, extra, 0)
    left_side = pad_axis(jnp.swapaxes(strips[..., 2, :, :, :], -3, -2), 2, 0, extra)
    right_side = pad_axis(jnp.flip(jnp.swapaxes(strips[..., 3, :, :, :], -3, -2), -2), 2, extra, 0)
    return top_side + bottom_side + left_side + right_side

def assemble(field_in, side_cells):
    top_block = jnp.flip(side_cells[..., 0, :, :, :], -3)
    bottom_block = side_cells[..., 1, :, :, :]
    left_block = jnp.flip(jnp.swapaxes(side_cells[..., 2, :, :, :], -3, -2), -2)
    right_block = jnp.swapaxes(side_cells[..., 3, :, :, :], -3, -2)
    middle = jnp.concatenate([left_block, field_in, right_block], -2)
    top_full = pad_axis(top_block, 2, HALO, HALO)
    bottom_full = pad_axis(bottom_block, 2, HALO, HALO)
    return jnp.concatenate([top_full, middle, bottom_full], -3)

def rim_cells(grad_padded_tile):
    edge_length = grad_padded_tile.shape[-2] - 2 * HALO
    inner = grad_padded_tile[..., HALO:HALO + edge_length, HALO:HALO + edge_length, :]
    top_side = jnp.flip(grad_padded_tile[..., :HALO, HALO:HALO + edge_length, :], -3)
    bottom_side = grad_padded_tile[..., HALO + edge_length:, HALO:HALO + edge_length, :]
    left_side = jnp.swapaxes(jnp.flip(grad_padded_tile[..., HALO:HALO + edge_length, :HALO, :], -2), -3, -2)
    right_side = jnp.swapaxes(grad_padded_tile[..., HALO:HALO + edge_length, HALO + edge_length:, :], -3, -2)
    return (inner, jnp.stack([top_side, bottom_side, left_side, right_side], -4))

def depthwise(padded_tile, kernel):
    edge_length = padded_tile.shape[-2] - 2 * HALO
    summed = jnp.zeros(padded_tile.shape[:-3] + (edge_length, edge_length, padded_tile.shape[-1]), jnp.float32)
    for first_operand in range(KERNEL_TAPS):
        for second_operand in range(KERNEL_TAPS):
            tap_window = padded_tile[..., DILATION_STEP * first_operand:DILATION_STEP * first_operand + edge_length, DILATION_STEP * second_operand:DILATION_STEP * second_operand + edge_length, :].astype(jnp.float32)
            summed = summed + tap_window * kernel[first_operand * KERNEL_TAPS + second_operand]
    return summed

def depthwise_back(grad_convolved, kernel):
    edge_length = grad_convolved.shape[-2]
    full_len = edge_length + 2 * HALO
    grad_padded_tile = jnp.zeros(grad_convolved.shape[:-3] + (full_len, full_len, grad_convolved.shape[-1]), jnp.float32)
    for first_operand in range(KERNEL_TAPS):
        for second_operand in range(KERNEL_TAPS):
            grad_padded_tile = grad_padded_tile.at[..., DILATION_STEP * first_operand:DILATION_STEP * first_operand + edge_length, DILATION_STEP * second_operand:DILATION_STEP * second_operand + edge_length, :].add(grad_convolved * kernel[first_operand * KERNEL_TAPS + second_operand])
    return grad_padded_tile

def tap_sums(padded_tile, grad_convolved):
    edge_length = grad_convolved.shape[-2]
    channels = grad_convolved.shape[-1]
    tap_rows = []
    for first_operand in range(KERNEL_TAPS):
        for second_operand in range(KERNEL_TAPS):
            tap_window = padded_tile[..., DILATION_STEP * first_operand:DILATION_STEP * first_operand + edge_length, DILATION_STEP * second_operand:DILATION_STEP * second_operand + edge_length, :].astype(jnp.float32)
            tap_rows.append(lax.optimization_barrier(jnp.sum((tap_window * grad_convolved).reshape(-1, channels), 0)))
    return jnp.stack(tap_rows)

def normalize(conv):
    mean_value = lax.optimization_barrier(jnp.mean(conv, -1, keepdims=True))
    centred = conv - mean_value
    inv_std = lax.rsqrt(lax.optimization_barrier(jnp.mean(centred * centred, -1, keepdims=True)) + 1e-06)
    return (centred * inv_std, inv_std)

def reference(features, cotangent, kernel, weight_in, weight_out, tile_neighbour, edge_code):
    source = (tile_neighbour * 4 + edge_code % 4).reshape(-1).astype(jnp.int32)
    flipped_mask = (edge_code >= 4)[:, :, None, None, None]
    norm_factor = 1.0 / math.sqrt(MEMBERS * TILES * TILE * TILE)

    def member_step(totals, inputs):
        field_in, grad_out = inputs
        strips = edge_strips(field_in, HALO).reshape(TILES * 4, HALO, TILE, C)
        side_cells = jnp.take(strips, source, axis=0).reshape(TILES, 4, HALO, TILE, C)
        side_cells = jnp.where(flipped_mask, jnp.flip(side_cells, -2), side_cells)
        padded_tile = assemble(field_in, side_cells)
        conv = depthwise(padded_tile, kernel)
        normed_f, inv_std = normalize(conv)
        normed = normed_f.astype(jnp.bfloat16).reshape(-1, C)
        preact = jnp.dot(normed, weight_in, preferred_element_type=jnp.float32)
        hidden = jax.nn.gelu(preact).astype(jnp.bfloat16)
        grad_rows = grad_out.reshape(-1, C)
        part_out = jnp.dot(hidden.T, grad_rows, preferred_element_type=jnp.float32)
        d_hidden = jnp.dot(grad_rows, weight_out.T, preferred_element_type=jnp.float32)
        _, pull_back = jax.vjp(jax.nn.gelu, preact)
        d_preact = pull_back(d_hidden)[0].astype(jnp.bfloat16)
        part_in = jnp.dot(normed.T, d_preact, preferred_element_type=jnp.float32)
        d_normed = jnp.dot(d_preact, weight_in.T, preferred_element_type=jnp.float32).reshape(conv.shape)
        grad_convolved = inv_std * (d_normed - lax.optimization_barrier(jnp.mean(d_normed, -1, keepdims=True)) - normed_f * lax.optimization_barrier(jnp.mean(d_normed * normed_f, -1, keepdims=True)))
        part_kernel = tap_sums(padded_tile, grad_convolved)
        grad_padded_tile = depthwise_back(grad_convolved, kernel)
        inner, side_grads = rim_cells(grad_padded_tile)
        side_grads = jnp.where(flipped_mask, jnp.flip(side_grads, -2), side_grads)
        edge_back = jax.ops.segment_sum(side_grads.reshape(TILES * 4, HALO, TILE, C), source, num_segments=TILES * 4)
        edge_back = edge_back.reshape(TILES, 4, HALO, TILE, C)
        grad_field = (grad_out.astype(jnp.float32) + inner + place_edges(edge_back, TILE)).astype(jnp.bfloat16)
        new_totals = (totals[0] + part_kernel, totals[1] + part_in, totals[2] + part_out)
        return (new_totals, grad_field)
    start = (jnp.zeros((KERNEL_TAPS * KERNEL_TAPS, C), jnp.float32), jnp.zeros((C, HID), jnp.float32), jnp.zeros((HID, C), jnp.float32))
    totals, grad_features = lax.scan(member_step, start, (features, cotangent))
    return (grad_features, totals[0] * norm_factor, totals[1] * norm_factor, totals[2] * norm_factor)
```

```python
import functools
import math

import jax
import jax.numpy as jnp
from jax import lax
from jax.experimental import pallas as pl
from jax.experimental.pallas import tpu as pltpu
from jax.sharding import PartitionSpec as P

C = 256
HID = 1024
TAPS = 7
STEP = 2
HALO = 6
N = 16
ROWS = N + 2 * HALO
LANES = 128
FRAME = 32
LEFT = 8
GROUP = 4
EXTRA = 16
F32 = jnp.float32
BF16 = jnp.bfloat16
GELU_A = math.sqrt(2.0 / math.pi)
GELU_B = 0.044715
VMEM = pl.BlockSpec(memory_space=pltpu.VMEM)
SMEM = pl.BlockSpec(memory_space=pltpu.SMEM)


def dot(a, b, ca, cb):
    return lax.dot_general(a, b, (((ca,), (cb,)), ((), ())), preferred_element_type=F32)


def tap_offset(b):
    return LEFT - HALO + STEP * b


def side_onehots(meta):
    parts = []
    for s in range(4):
        n = HALO * N if s < 2 else 8 * N
        rho = lax.broadcasted_iota(jnp.int32, (n, 1), 0)
        if s < 2:
            m = rho & (N - 1)
            k = rho >> 4
            if s == 0:
                k = HALO - 1 - k
            ok = None
        else:
            m = rho >> 3
            q = rho & 7
            k = LEFT - 1 - q if s == 2 else q
            ok = k < HALO
        target = meta[3 * s] + meta[3 * s + 1] * k + meta[3 * s + 2] * m
        if ok is not None:
            target = jnp.where(ok, target, -1)
        lane = lax.broadcasted_iota(jnp.int32, (n, 3 * N * N), 1)
        parts.append(jnp.where(target == lane, 1.0, 0.0).astype(BF16))
    return parts


def fill_frame(meta, own_ref, one_ref, two_ref, frame):
    own = own_ref[...]
    zero_cols = jnp.zeros((HALO, LEFT, LANES), F32)
    onehots = side_onehots(meta)
    rims = [
        dot(s[:, : N * N], own, 1, 0)
        + dot(s[:, N * N : 2 * N * N], one_ref[...], 1, 0)
        + dot(s[:, 2 * N * N :], two_ref[...], 1, 0)
        for s in onehots
    ]
    inner = own.astype(F32).reshape(N, N, C)
    for l in range(C // LANES):
        lanes = slice(l * LANES, (l + 1) * LANES)
        for top in (0, HALO + N):
            for left in (0, LEFT + N):
                frame[l, top : top + HALO, left : left + LEFT, :] = zero_cols
        frame[l, :HALO, LEFT : LEFT + N, :] = rims[0][:, lanes].reshape(HALO, N, LANES)
        frame[l, HALO + N :, LEFT : LEFT + N, :] = rims[1][:, lanes].reshape(HALO, N, LANES)
        frame[l, HALO : HALO + N, :LEFT, :] = rims[2][:, lanes].reshape(N, 8, LANES)
        frame[l, HALO : HALO + N, LEFT + N :, :] = rims[3][:, lanes].reshape(N, 8, LANES)
        frame[l, HALO : HALO + N, LEFT : LEFT + N, :] = inner[:, :, lanes]


def forward_kernel(
    meta, core, own_ref, one_ref, two_ref, cot_ref, taps_ref, win_ref, wout_ref,
    send_ref, keep_ref, dconv_ref, frame, conv,
):
    fill_frame(meta, own_ref, one_ref, two_ref, frame)
    for l in range(C // LANES):
        lanes = slice(l * LANES, (l + 1) * LANES)
        acc = [None] * N
        for b in range(TAPS):
            off = tap_offset(b)
            coef = [taps_ref[a * TAPS + b : a * TAPS + b + 1, lanes] for a in range(TAPS)]
            for r in range(ROWS):
                x = frame[l, r, off : off + N, :]
                for a in range(TAPS):
                    i = r - STEP * a
                    if 0 <= i < N:
                        term = x * coef[a]
                        acc[i] = term if acc[i] is None else acc[i] + term
        for i in range(N):
            conv[i * N : (i + 1) * N, lanes] = acc[i]
    value = conv[...]
    centred = value - jnp.mean(value, -1, keepdims=True)
    inv_std = lax.rsqrt(jnp.mean(centred * centred, -1, keepdims=True) + 1e-06)
    normed_f = centred * inv_std
    normed = normed_f.astype(BF16)
    cot = cot_ref[...]
    first = core[0] == 0
    d_normed = None
    for h in range(GROUP):
        cols = slice(h * C, (h + 1) * C)
        w_in = win_ref[:, cols]
        pre = dot(normed, w_in, 1, 0)
        d_hidden = dot(cot, wout_ref[cols, :], 1, 1)
        square = pre * pre
        t = jnp.tanh(pre * (GELU_A + (GELU_A * GELU_B) * square))
        half = 0.5 + 0.5 * t
        hidden = (pre * half).astype(BF16)
        slope = half + (0.5 * pre) * (1.0 - t * t) * (GELU_A + (3.0 * GELU_A * GELU_B) * square)
        d_pre = (d_hidden * slope).astype(BF16)
        part_out = dot(hidden, cot, 0, 0).astype(BF16)
        part_in = dot(normed, d_pre, 0, 0).astype(BF16)
        send_ref[h] = jnp.where(first, part_out, part_in)
        keep_ref[h] = jnp.where(first, part_in, part_out)
        back = dot(d_pre, w_in, 1, 1)
        d_normed = back if d_normed is None else d_normed + back
    dconv_ref[...] = inv_std * (
        d_normed
        - jnp.mean(d_normed, -1, keepdims=True)
        - normed_f * jnp.mean(d_normed * normed_f, -1, keepdims=True)
    )


def taps_kernel(meta, own_ref, one_ref, two_ref, dconv_ref, out_ref, frame):
    fill_frame(meta, own_ref, one_ref, two_ref, frame)
    out_ref[...] = jnp.zeros(out_ref.shape, F32)
    for l in range(C // LANES):
        lanes = slice(l * LANES, (l + 1) * LANES)
        grad = [dconv_ref[i * N : (i + 1) * N, lanes] for i in range(N)]
        for b in range(TAPS):
            off = tap_offset(b)
            acc = [None] * TAPS
            for r in range(ROWS):
                x = frame[l, r, off : off + N, :]
                for a in range(TAPS):
                    i = r - STEP * a
                    if 0 <= i < N:
                        term = x * grad[i]
                        acc[a] = term if acc[a] is None else acc[a] + term
            for a in range(TAPS):
                t = a * TAPS + b
                out_ref[t // EXTRA, t % EXTRA : t % EXTRA + 1, lanes] = jnp.sum(
                    acc[a], 0, keepdims=True
                )


def backward_kernel(meta, dconv_ref, taps_ref, cot_ref, own_ref, one_ref, two_ref, shifted, rim):
    residues = (2, 4, 6, 0)
    pad = jnp.zeros((ROWS, 8, LANES), F32)
    for l in range(C // LANES):
        lanes = slice(l * LANES, (l + 1) * LANES)
        grad = [
            [dconv_ref[i * N + 8 * t : i * N + 8 * t + 8, lanes] for t in range(2)]
            for i in range(N)
        ]
        for n, s in enumerate(residues):
            shifted[l, n, :, 0:8, :] = pad
            shifted[l, n, :, 32:40, :] = pad
            pieces = [(b, tap_offset(b) // 8) for b in range(TAPS) if tap_offset(b) % 8 == s]
            coef = {
                (a, b): taps_ref[a * TAPS + b : a * TAPS + b + 1, lanes]
                for a in range(TAPS)
                for b, _ in pieces
            }
            for r in range(ROWS):
                acc = [None] * 3
                for a in range(TAPS):
                    i = r - STEP * a
                    if 0 <= i < N:
                        for b, up in pieces:
                            for t in range(2):
                                term = grad[i][t] * coef[a, b]
                                acc[t + up] = term if acc[t + up] is None else acc[t + up] + term
                for t in range(3):
                    shifted[l, n, r, 8 + 8 * t : 16 + 8 * t, :] = (
                        jnp.zeros((8, LANES), F32) if acc[t] is None else acc[t]
                    )

        def gather(rows, first_col, count):
            total = None
            for n, s in enumerate(residues):
                at = 8 + first_col - s
                piece = shifted[l, n, rows, at : at + count, :]
                total = piece if total is None else total + piece
            return total

        top = gather(slice(0, HALO), LEFT, N)
        bottom = gather(slice(HALO + N, ROWS), LEFT, N)
        middle = slice(HALO, HALO + N)
        left = gather(middle, 0, 8)
        right = gather(middle, LEFT + N, 8)
        inner = gather(middle, LEFT, N)
        at = 0
        for block in (top, bottom, left, right):
            n = block.shape[0] * block.shape[1]
            rim[at : at + n, lanes] = block.reshape(n, LANES).astype(BF16)
            at += n
        own_ref[:, lanes] = inner.reshape(N * N, LANES) + cot_ref[:, lanes].astype(F32)
    onehot = jnp.concatenate(side_onehots(meta), 0)
    cells = rim[...]
    own_ref[...] += dot(onehot[:, : N * N], cells, 0, 0)
    one_ref[...] = dot(onehot[:, N * N : 2 * N * N], cells, 0, 0).astype(BF16)
    two_ref[...] = dot(onehot[:, 2 * N * N :], cells, 0, 0).astype(BF16)


def spread_kernel(place, keep_ref, got_ref, taps_ref, own_ref, one_ref, two_ref, three_ref):
    for d, out in enumerate((own_ref, one_ref, two_ref, three_ref)):
        j = place[0] ^ d
        out[:C, :] = (keep_ref[j].astype(F32) + got_ref[j].astype(F32)).astype(out.dtype)
        out[C:, :] = taps_ref[j].astype(out.dtype)


def finish_kernel(scale, place, core, *refs):
    mine, theirs = refs[:GROUP], refs[GROUP : 2 * GROUP]
    kernel_ref, in_ref, out_ref, rows = refs[2 * GROUP :]
    first = core[0] == 0
    for d in range(GROUP):
        j = place[0] ^ d
        at = pl.multiple_of(j * C, C)
        a = mine[d][:C, :]
        b = theirs[d][:C, :]
        in_ref[:, pl.ds(at, C)] = jnp.where(first, a, b).astype(F32) * scale
        out_ref[pl.ds(at, C), :] = jnp.where(first, b, a).astype(F32) * scale
        rows[j] = (mine[d][C:, :].astype(F32) + theirs[d][C:, :].astype(F32)) * scale
    for j in range(GROUP):
        n = min(EXTRA, TAPS * TAPS - j * EXTRA)
        kernel_ref[j * EXTRA : j * EXTRA + n, :] = rows[j, :n, :]


def call(kernel, outs, scratch=(), specs=(), flops=0, nbytes=0, vmem=48):
    return pl.pallas_call(
        kernel,
        out_shape=outs,
        in_specs=specs,
        out_specs=jax.tree.map(lambda _: VMEM, outs),
        scratch_shapes=scratch,
        compiler_params=pltpu.CompilerParams(vmem_limit_bytes=vmem * 1024 * 1024),
        cost_estimate=pl.CostEstimate(flops=flops, bytes_accessed=nbytes, transcendentals=0),
    )


def body(features, cotangent, kernel, weight_in, weight_out, tile_neighbour, edge_code):
    owners = lax.axis_size("tile")
    members = lax.axis_size("ens")
    position = lax.axis_index("tile")
    member = lax.axis_index("ens")
    devices = owners * members
    scale = 1.0 / math.sqrt(devices * N * N)
    both = ("tile", "ens")
    struct = jax.ShapeDtypeStruct

    def swap(x, bits):
        return lax.ppermute(x, both, [(i, i ^ bits) for i in range(devices)])

    def one_over(x):
        return lax.ppermute(x, "tile", [(i, i ^ 1) for i in range(owners)])

    def two_over(x):
        moves = [(i, (i + 1 if i % 2 else i - 1) % owners) for i in range(owners)]
        return lax.ppermute(x, "tile", moves)

    offset = (tile_neighbour[0] - position + 1) % owners
    odd = position % 2
    source = jnp.where(offset == 1, 0, jnp.where((offset == 0) == (odd == 1), 1, 2))
    edge = edge_code[0] % 4
    flipped = edge_code[0] // 4 % 2
    along = jnp.where(edge < 2, 1, N)
    across = jnp.where(edge < 2, N, 1)
    base = source * (N * N) + flipped * (N - 1) * along + (edge % 2) * (N - 1) * across
    step_k = across * (1 - 2 * (edge % 2))
    step_m = along * (1 - 2 * flipped)
    meta = jnp.stack([base, step_k, step_m], -1).reshape(-1).astype(jnp.int32)
    core = (member % 2).reshape(1).astype(jnp.int32)
    place = ((member // 2) % 2 + 2 * (position % 2)).reshape(1).astype(jnp.int32)

    own = features.reshape(N * N, C)
    cot = cotangent.reshape(N * N, C)
    two = two_over(own)
    one = one_over(own)

    frame = pltpu.VMEM((2, ROWS, FRAME, LANES), F32)
    send, keep, dconv = call(
        forward_kernel,
        (struct((GROUP, C, C), BF16), struct((GROUP, C, C), BF16), struct((N * N, C), F32)),
        [frame, pltpu.VMEM((N * N, C), F32)],
        [SMEM] * 2 + [VMEM] * 7,
        flops=700_000_000,
        nbytes=4_000_000,
    )(meta, core, own, one, two, cot, kernel, weight_in, weight_out)
    got = swap(send, 1)
    part_taps = call(
        taps_kernel,
        struct((GROUP, EXTRA, C), F32),
        [frame],
        [SMEM] + [VMEM] * 4,
        nbytes=6_000_000,
    )(meta, own, one, two, dconv)

    block = struct((C + EXTRA, C), BF16)
    pieces = call(
        spread_kernel, (block,) * GROUP, (), [SMEM] + [VMEM] * 3, nbytes=3_000_000
    )(place, keep, got, part_taps)
    square = [2, members, 2 + members]
    total = pieces[0].astype(F32)
    for piece, bits in zip(pieces[1:], square):
        total = total + swap(piece, bits).astype(F32)
    total = total.astype(BF16)

    grad_own, grad_one, grad_two = call(
        backward_kernel,
        (struct((N * N, C), F32), struct((N * N, C), BF16), struct((N * N, C), BF16)),
        [pltpu.VMEM((2, 4, ROWS, 40, LANES), F32), pltpu.VMEM((28 * N, C), BF16)],
        [SMEM] + [VMEM] * 3,
        nbytes=10_000_000,
    )(meta, dconv, kernel, cot)

    rest = [1 << n for n in range(2, members.bit_length() - 1)]
    rest += [members << n for n in range(1, owners.bit_length() - 1)]
    while rest:
        bits, rest = rest[:2], rest[2:]
        if len(bits) == 2:
            a, b = bits
            far, near, mid = swap(total, a + b), swap(total, a), swap(total, b)
            total = (total.astype(F32) + near.astype(F32)) + (mid.astype(F32) + far.astype(F32))
        else:
            total = total.astype(F32) + swap(total, bits[0]).astype(F32)
        total = total.astype(BF16)

    back_two = two_over(grad_two)
    back_one = one_over(grad_one)
    grad_features = (grad_own + back_one.astype(F32) + back_two.astype(F32)).astype(BF16)

    mine = [total] + [swap(total, bits) for bits in square]
    theirs = [swap(x, 1) for x in mine]
    grad_kernel, grad_in, grad_out = call(
        functools.partial(finish_kernel, scale),
        (struct((TAPS * TAPS, C), F32), struct((C, HID), F32), struct((HID, C), F32)),
        [pltpu.VMEM((GROUP, EXTRA, C), F32)],
        [SMEM] * 2 + [VMEM] * 8,
        nbytes=4_000_000,
    )(place, core, *mine, *theirs)
    return grad_features.reshape(features.shape), grad_kernel, grad_in, grad_out


def solution(mesh):
    halved = P("ens", "tile", None, None, None)
    in_specs = (halved, halved, P(), P(), P(), P("tile", None), P("tile", None))
    out_specs = (halved, P(), P(), P())
    return jax.shard_map(body, mesh=mesh, in_specs=in_specs, out_specs=out_specs, check_vma=False)
```

```python
import functools
import math

import jax
import jax.numpy as jnp
from jax import lax
from jax.experimental import pallas as pl
from jax.experimental.pallas import tpu as pltpu
from jax.sharding import PartitionSpec as P

C = 256
HID = 1024
TAPS = 7
STEP = 2
HALO = 6
N = 16
ROWS = N + 2 * HALO
LANES = 128
FRAME = 32
LEFT = 8
GROUP = 4
JOIN_COST = 30_000_000_000
EXTRA = 16
F32 = jnp.float32
BF16 = jnp.bfloat16
GELU_A = math.sqrt(2.0 / math.pi)
GELU_B = 0.044715
SIDE_CELLS = 2 * HALO * N + 2 * LEFT * N
RIMS = (
    (slice(0, HALO), slice(LEFT, LEFT + N), slice(0, 96)),
    (slice(HALO + N, ROWS), slice(LEFT, LEFT + N), slice(96, 192)),
    (slice(HALO, HALO + N), slice(0, LEFT), slice(192, 320)),
    (slice(HALO, HALO + N), slice(LEFT + N, FRAME), slice(320, 448)),
)
VMEM = pl.BlockSpec(memory_space=pltpu.VMEM)
ANY = pl.BlockSpec(memory_space=pl.ANY)
HBM = pl.BlockSpec(memory_space=pltpu.HBM)
SMEM = pl.BlockSpec(memory_space=pltpu.SMEM)


def span(s):
    return s.stop - s.start


def dot(a, b, ca, cb):
    return lax.dot_general(a, b, (((ca,), (cb,)), ((), ())), preferred_element_type=F32)


def tap_offset(b):
    return LEFT - HALO + STEP * b


def span(s):
    return s.stop - s.start


def side_targets(owners, neighbour, code, position):
    targets = []
    for s in range(4):
        offset = lax.rem(neighbour[0, s] - position + 1 + owners, owners)
        first = (offset == 0) == (lax.rem(position, 2) == 1)
        source = jnp.where(offset == 1, 0, jnp.where(first, 1, 2))
        edge = code[0, s] & 3
        flipped = (code[0, s] >> 2) & 1
        along = jnp.where(edge < 2, 1, N)
        across = jnp.where(edge < 2, N, 1)
        far = edge & 1
        base = source * (N * N) + flipped * (N - 1) * along + far * (N - 1) * across
        step_k = across * (1 - 2 * far)
        step_m = along * (1 - 2 * flipped)
        n = HALO * N if s < 2 else LEFT * N
        rho = lax.broadcasted_iota(jnp.int32, (n, 1), 0)
        if s < 2:
            m = rho & (N - 1)
            k = rho >> 4
            if s == 0:
                k = HALO - 1 - k
            targets.append(base + step_k * k + step_m * m)
        else:
            m = rho >> 3
            q = rho & (LEFT - 1)
            k = LEFT - 1 - q if s == 2 else q
            targets.append(jnp.where(k < HALO, base + step_k * k + step_m * m, -1))
    return jnp.concatenate(targets, 0)


def prepare_kernel(
    owners, neighbour, code, position, own_hbm, cot_hbm, taps_hbm, win_hbm, wout_hbm,
    onehot, frame, d_hidden, cot_ref, taps_ref, win_ref, own_ref, wout_ref, sems,
):
    copies = [
        pltpu.make_async_copy(src, dst, sems.at[n])
        for n, (src, dst) in enumerate(
            (
                (own_hbm, own_ref),
                (cot_hbm, cot_ref),
                (wout_hbm, wout_ref),
                (win_hbm, win_ref),
                (taps_hbm, taps_ref),
            )
        )
    ]
    for copy in copies:
        copy.start()
    target = side_targets(owners, neighbour, code, position[0])
    lane = lax.broadcasted_iota(jnp.int32, (SIDE_CELLS, 3 * N * N), 1)
    onehot[...] = jnp.where(target == lane, 1.0, 0.0).astype(BF16)
    corner = jnp.zeros((HALO, LEFT, LANES), F32)
    copies[0].wait()
    own = own_ref[...]
    rims = dot(onehot[:, : N * N], own, 1, 0)
    inner = own.astype(F32).reshape(N, N, C)
    for l in range(C // LANES):
        lanes = slice(l * LANES, (l + 1) * LANES)
        for top in (0, HALO + N):
            for left in (0, LEFT + N):
                frame[l, top : top + HALO, left : left + LEFT, :] = corner
        for rows, cols, cells in RIMS:
            frame[l, rows, cols, :] = rims[cells, lanes].reshape(span(rows), span(cols), LANES)
        frame[l, HALO : HALO + N, LEFT : LEFT + N, :] = inner[:, :, lanes]
    copies[1].wait()
    copies[2].wait()
    d_hidden[...] = dot(cot_ref[...], wout_ref[...], 1, 1)
    copies[3].wait()
    copies[4].wait()


def add_rims(cells_to, tile_ref, onehot, frame):
    rims = dot(onehot[:, cells_to], tile_ref[...], 1, 0)
    for l in range(C // LANES):
        lanes = slice(l * LANES, (l + 1) * LANES)
        for rows, cols, cells in RIMS:
            frame[l, rows, cols, :] += rims[cells, lanes].reshape(span(rows), span(cols), LANES)


def one_kernel(start_ref, one_ref, onehot, frame):
    del start_ref
    add_rims(slice(N * N, 2 * N * N), one_ref, onehot, frame)


def forward_kernel(
    core, start_ref, two_ref, onehot, d_hidden_ref, cot_ref, taps_ref, win_ref,
    send_ref, keep_ref, dconv_ref, frame, conv,
):
    del start_ref
    add_rims(slice(2 * N * N, 3 * N * N), two_ref, onehot, frame)
    for l in range(C // LANES):
        lanes = slice(l * LANES, (l + 1) * LANES)
        acc = [None] * N
        for b in range(TAPS):
            off = tap_offset(b)
            coef = [taps_ref[a * TAPS + b : a * TAPS + b + 1, lanes] for a in range(TAPS)]
            for r in range(ROWS):
                x = frame[l, r, off : off + N, :]
                for a in range(TAPS):
                    i = r - STEP * a
                    if 0 <= i < N:
                        term = x * coef[a]
                        acc[i] = term if acc[i] is None else acc[i] + term
        for i in range(N):
            conv[i * N : (i + 1) * N, lanes] = acc[i]
    value = conv[...]
    centred = value - jnp.mean(value, -1, keepdims=True)
    inv_std = lax.rsqrt(jnp.mean(centred * centred, -1, keepdims=True) + 1e-06)
    normed_f = centred * inv_std
    normed = normed_f.astype(BF16)
    cot = cot_ref[...]
    first = core[0] == 0
    d_normed = None
    for h in range(GROUP):
        cols = slice(h * C, (h + 1) * C)
        w_in = win_ref[:, cols]
        pre = dot(normed, w_in, 1, 0)
        square = pre * pre
        t = jnp.tanh(pre * (GELU_A + (GELU_A * GELU_B) * square))
        half = 0.5 + 0.5 * t
        hidden = (pre * half).astype(BF16)
        slope = half + (0.5 * pre) * (1.0 - t * t) * (GELU_A + (3.0 * GELU_A * GELU_B) * square)
        d_pre = (d_hidden_ref[:, cols] * slope).astype(BF16)
        part_out = dot(hidden, cot, 0, 0).astype(BF16)
        part_in = dot(normed, d_pre, 0, 0).astype(BF16)
        send_ref[h] = jnp.where(first, part_out, part_in)
        keep_ref[h] = jnp.where(first, part_in, part_out)
        back = dot(d_pre, w_in, 1, 1)
        d_normed = back if d_normed is None else d_normed + back
    dconv_ref[...] = inv_std * (
        d_normed
        - jnp.mean(d_normed, -1, keepdims=True)
        - normed_f * jnp.mean(d_normed * normed_f, -1, keepdims=True)
    )


def taps_kernel(frame, dconv_ref, out_ref):
    out_ref[...] = jnp.zeros(out_ref.shape, F32)
    for l in range(C // LANES):
        lanes = slice(l * LANES, (l + 1) * LANES)
        grad = [dconv_ref[i * N : (i + 1) * N, lanes] for i in range(N)]
        for b in range(TAPS):
            off = tap_offset(b)
            acc = [None] * TAPS
            for r in range(ROWS):
                x = frame[l, r, off : off + N, :]
                for a in range(TAPS):
                    i = r - STEP * a
                    if 0 <= i < N:
                        term = x * grad[i]
                        acc[a] = term if acc[a] is None else acc[a] + term
            for a in range(TAPS):
                t = a * TAPS + b
                out_ref[t // EXTRA, t % EXTRA : t % EXTRA + 1, lanes] = jnp.sum(
                    acc[a], 0, keepdims=True
                )


def backward_kernel(onehot, dconv_ref, taps_ref, cot_ref, own_ref, one_ref, two_ref, shifted, rim):
    residues = (2, 4, 6, 0)
    pad = jnp.zeros((ROWS, 8, LANES), F32)
    for l in range(C // LANES):
        lanes = slice(l * LANES, (l + 1) * LANES)
        grad = [
            [dconv_ref[i * N + 8 * t : i * N + 8 * t + 8, lanes] for t in range(2)]
            for i in range(N)
        ]
        for n, s in enumerate(residues):
            shifted[l, n, :, 0:8, :] = pad
            shifted[l, n, :, 32:40, :] = pad
            pieces = [(b, tap_offset(b) // 8) for b in range(TAPS) if tap_offset(b) % 8 == s]
            coef = {
                (a, b): taps_ref[a * TAPS + b : a * TAPS + b + 1, lanes]
                for a in range(TAPS)
                for b, _ in pieces
            }
            for r in range(ROWS):
                acc = [None] * 3
                for a in range(TAPS):
                    i = r - STEP * a
                    if 0 <= i < N:
                        for b, up in pieces:
                            for t in range(2):
                                term = grad[i][t] * coef[a, b]
                                acc[t + up] = term if acc[t + up] is None else acc[t + up] + term
                for t in range(3):
                    shifted[l, n, r, 8 + 8 * t : 16 + 8 * t, :] = (
                        jnp.zeros((8, LANES), F32) if acc[t] is None else acc[t]
                    )

        def gather(rows, first_col, count):
            total = None
            for n, s in enumerate(residues):
                at = 8 + first_col - s
                piece = shifted[l, n, rows, at : at + count, :]
                total = piece if total is None else total + piece
            return total

        top = gather(slice(0, HALO), LEFT, N)
        bottom = gather(slice(HALO + N, ROWS), LEFT, N)
        middle = slice(HALO, HALO + N)
        left = gather(middle, 0, 8)
        right = gather(middle, LEFT + N, 8)
        inner = gather(middle, LEFT, N)
        at = 0
        for block in (top, bottom, left, right):
            n = block.shape[0] * block.shape[1]
            rim[at : at + n, lanes] = block.reshape(n, LANES).astype(BF16)
            at += n
        own_ref[:, lanes] = inner.reshape(N * N, LANES) + cot_ref[:, lanes].astype(F32)
    cells = rim[...]
    own_ref[...] += dot(onehot[:, : N * N], cells, 0, 0)
    one_ref[...] = dot(onehot[:, N * N : 2 * N * N], cells, 0, 0).astype(BF16)
    two_ref[...] = dot(onehot[:, 2 * N * N :], cells, 0, 0).astype(BF16)


def spread_kernel(place, keep_ref, got_ref, taps_ref, own_ref, one_ref, two_ref, three_ref):
    for d, out in enumerate((own_ref, one_ref, two_ref, three_ref)):
        j = place[0] ^ d
        out[:C, :] = (keep_ref[j].astype(F32) + got_ref[j].astype(F32)).astype(out.dtype)
        out[C:, :] = taps_ref[j].astype(out.dtype)


def store_blocks(scale, to_in, place, blocks, in_hbm, out_hbm, stage, sems):
    copies = []
    for d in range(GROUP):
        stage[d] = blocks[d][:C, :].astype(F32) * scale
        at = pl.ds(pl.multiple_of((place ^ d) * C, C), C)
        into_in = pltpu.make_async_copy(stage.at[d], in_hbm.at[:, at], sems.at[d])
        into_out = pltpu.make_async_copy(stage.at[d], out_hbm.at[at, :], sems.at[d])
        pl.when(to_in)(into_in.start)
        pl.when(jnp.logical_not(to_in))(into_out.start)
        copies.append((into_in, into_out))
    return copies


def wait_blocks(to_in, copies):
    for into_in, into_out in copies:
        pl.when(to_in)(into_in.wait)
        pl.when(jnp.logical_not(to_in))(into_out.wait)


def finish_mine_kernel(scale, core, place, *refs):
    blocks = refs[:GROUP]
    in_hbm, out_hbm, rows, stage, sems = refs[GROUP:]
    to_in = core[0] == 0
    copies = store_blocks(scale, to_in, place[0], blocks, in_hbm, out_hbm, stage, sems)
    for d in range(GROUP):
        rows[place[0] ^ d] = blocks[d][C:, :].astype(F32)
    wait_blocks(to_in, copies)


def finish_theirs_kernel(scale, core, place, *refs):
    blocks, (mine_ref, _, _) = refs[:GROUP], refs[GROUP : GROUP + 3]
    in_hbm, out_hbm, kernel_ref, rows, stage, sems = refs[GROUP + 3 :]
    to_in = core[0] != 0
    copies = store_blocks(scale, to_in, place[0], blocks, in_hbm, out_hbm, stage, sems)
    for d in range(GROUP):
        rows[place[0] ^ d] = blocks[d][C:, :].astype(F32)
    for j in range(GROUP):
        n = min(EXTRA, TAPS * TAPS - j * EXTRA)
        kernel_ref[j * EXTRA : j * EXTRA + n, :] = (mine_ref[j, :n, :] + rows[j, :n, :]) * scale
    wait_blocks(to_in, copies)


def join_kernel(own_ref, one_ref, two_ref, out_ref):
    out_ref[...] = (own_ref[...] + one_ref[...].astype(F32) + two_ref[...].astype(F32)).astype(BF16)


def in_hbm(x):
    return pltpu.with_memory_space_constraint(x, pltpu.HBM)


def call(kernel, outs, scratch=(), specs=(), flops=0, aliases={}, out_specs=None, vmem=16):
    return pl.pallas_call(
        kernel,
        out_shape=outs,
        in_specs=specs,
        out_specs=out_specs or jax.tree.map(lambda _: VMEM, outs),
        scratch_shapes=scratch,
        input_output_aliases=aliases,
        compiler_params=pltpu.CompilerParams(vmem_limit_bytes=vmem * 1024 * 1024),
        cost_estimate=pl.CostEstimate(flops=flops, bytes_accessed=0, transcendentals=0),
    )


def body(features, cotangent, kernel, weight_in, weight_out, tile_neighbour, edge_code):
    owners = lax.axis_size("tile")
    members = lax.axis_size("ens")
    position = lax.axis_index("tile")
    member = lax.axis_index("ens")
    devices = owners * members
    scale = 1.0 / math.sqrt(devices * N * N)
    both = ("tile", "ens")
    struct = jax.ShapeDtypeStruct

    def one_over(x):
        return lax.ppermute(x, "tile", [(i, i ^ 1) for i in range(owners)])

    def two_over(x):
        moves = [(i, (i + 1 if i % 2 else i - 1) % owners) for i in range(owners)]
        return lax.ppermute(x, "tile", moves)

    index = position * members + member
    free = [1 << n for n in range(2, members.bit_length() - 1)]
    free += [members << n for n in range(1, owners.bit_length() - 1)]
    pairs = ((2, members), (free[0], free[1]))
    later = [tuple(free[n : n + 2]) for n in range(2, len(free), 2)]

    def swap(x, even, odd):
        return lax.ppermute(x, both, [(i, i ^ (odd if i % 2 else even)) for i in range(devices)])

    def digit(pair):
        return jnp.where(index & pair[0], 1, 0) + jnp.where(index & pair[1], 2, 0)

    core = member % 2
    digits = (digit(pairs[0]), digit(pairs[1]))
    mine_at = jnp.where(core == 0, digits[0], digits[1]).astype(jnp.int32).reshape(1)
    theirs_at = jnp.where(core == 0, digits[1], digits[0]).astype(jnp.int32).reshape(1)
    core = core.reshape(1).astype(jnp.int32)
    combos = [[p[0], p[1], p[0] + p[1]] for p in pairs]

    own = features.reshape(N * N, C)
    one = one_over(own)
    two = two_over(own)

    frame = pltpu.VMEM((2, ROWS, FRAME, LANES), F32)
    onehot, frame_one, d_hidden, cot, taps, w_in = call(
        functools.partial(prepare_kernel, owners),
        (
            pltpu.VMEM((SIDE_CELLS, 3 * N * N), BF16),
            frame,
            pltpu.VMEM((N * N, HID), F32),
            pltpu.VMEM((N * N, C), BF16),
            pltpu.VMEM((TAPS * TAPS, C), F32),
            pltpu.VMEM((C, HID), BF16),
        ),
        [
            pltpu.VMEM((N * N, C), BF16),
            pltpu.VMEM((HID, C), BF16),
            pltpu.SemaphoreType.DMA((5,)),
        ],
        [SMEM] * 3 + [HBM] * 5,
    )(
        tile_neighbour, edge_code, position.reshape(1).astype(jnp.int32),
        *map(in_hbm, (own, cotangent.reshape(N * N, C), kernel, weight_in, weight_out)),
    )
    frame_one = call(
        one_kernel, frame, (), [VMEM] * 3, aliases={0: 0}
    )(frame_one, one, onehot)
    half = pltpu.VMEM((GROUP, C, C), BF16)
    send, keep, dconv, frame_two = call(
        forward_kernel,
        (half, half, pltpu.VMEM((N * N, C), F32), frame),
        [pltpu.VMEM((N * N, C), F32)],
        [SMEM] + [VMEM] * 7,
        aliases={1: 3},
    )(core, frame_one, two, onehot, d_hidden, cot, taps, w_in)
    got = swap(send, 1, 1)
    part_taps = call(
        taps_kernel, pltpu.VMEM((GROUP, EXTRA, C), F32), (), [VMEM] * 2
    )(frame_two, dconv)

    block = struct((C + EXTRA, C), BF16)
    pieces = call(
        spread_kernel, (block,) * GROUP, (), [SMEM] + [VMEM] * 3
    )(mine_at, keep, got, part_taps)
    total = pieces[0].astype(F32)
    for piece, even, odd in zip(pieces[1:], *combos):
        total = total + swap(piece, even, odd).astype(F32)
    total = total.astype(BF16)

    grad_own, grad_one, grad_two = call(
        backward_kernel,
        (pltpu.VMEM((N * N, C), F32), pltpu.VMEM((N * N, C), BF16), pltpu.VMEM((N * N, C), BF16)),
        [pltpu.VMEM((2, 4, ROWS, 40, LANES), F32), pltpu.VMEM((28 * N, C), BF16)],
        [VMEM] * 4,
    )(onehot, dconv, taps, cot)
    total, grad_one, grad_two = lax.optimization_barrier((total, grad_one, grad_two))

    back_two = two_over(grad_two)
    back_one = one_over(grad_one)
    for even, odd in [(pairs[1], pairs[0])] + [(p, p) for p in later]:
        got = [swap(total, a, b) for a, b in zip(even, odd)]
        summed = total.astype(F32) + got[0].astype(F32)
        if len(got) == 2:
            third = swap(total, sum(even), sum(odd))
            summed = summed + (got[1].astype(F32) + third.astype(F32))
        total = summed.astype(BF16)
    mine = [total] + [swap(total, even, odd) for even, odd in zip(*combos)]
    grad_features = call(
        join_kernel, struct((N * N, C), BF16), (), [VMEM] * 3, flops=JOIN_COST
    )(grad_own, back_one, back_two)
    mine, grad_features = lax.optimization_barrier((mine, grad_features))
    theirs = [swap(x, 1, 1) for x in mine]
    grads = (struct((C, HID), F32), struct((HID, C), F32))
    rows = struct((GROUP, EXTRA, C), F32)
    stage = [pltpu.VMEM((GROUP, C, C), F32), pltpu.SemaphoreType.DMA((GROUP,))]
    grad_in, grad_out, rows_mine = call(
        functools.partial(finish_mine_kernel, scale),
        (*grads, rows),
        stage,
        [SMEM] * 2 + [VMEM] * GROUP,
        out_specs=(ANY, ANY, VMEM),
    )(core, mine_at, *mine)
    grad_in, grad_out, grad_kernel = call(
        functools.partial(finish_theirs_kernel, scale),
        (*grads, struct((TAPS * TAPS, C), F32)),
        [pltpu.VMEM((GROUP, EXTRA, C), F32)] + stage,
        [SMEM] * 2 + [VMEM] * (GROUP + 1) + [ANY] * 2,
        out_specs=(ANY, ANY, VMEM),
        aliases={GROUP + 3: 0, GROUP + 4: 1},
    )(core, theirs_at, *theirs, rows_mine, grad_in, grad_out)
    return grad_features.reshape(features.shape), grad_kernel, grad_in, grad_out


def solution(mesh):
    halved = P("ens", "tile", None, None, None)
    in_specs = (halved, halved, P(), P(), P(), P("tile", None), P("tile", None))
    out_specs = (halved, P(), P(), P())
    return jax.shard_map(body, mesh=mesh, in_specs=in_specs, out_specs=out_specs, check_vma=False)
```

```python
import functools
import math

import jax
import jax.numpy as jnp
from jax import lax
from jax.experimental import pallas as pl
from jax.experimental.pallas import tpu as pltpu
from jax.sharding import PartitionSpec as P

C = 256
HID = 1024
TAPS = 7
STEP = 2
HALO = 6
N = 16
ROWS = N + 2 * HALO
LANES = 128
FRAME = 32
LEFT = 8
GROUP = 4
JOIN_COST = 30_000_000_000
EXTRA = 16
F32 = jnp.float32
BF16 = jnp.bfloat16
GELU_A = math.sqrt(2.0 / math.pi)
GELU_B = 0.044715
SIDE_CELLS = 2 * HALO * N + 2 * LEFT * N
RIMS = (
    (slice(0, HALO), slice(LEFT, LEFT + N), slice(0, 96)),
    (slice(HALO + N, ROWS), slice(LEFT, LEFT + N), slice(96, 192)),
    (slice(HALO, HALO + N), slice(0, LEFT), slice(192, 320)),
    (slice(HALO, HALO + N), slice(LEFT + N, FRAME), slice(320, 448)),
)
VMEM = pl.BlockSpec(memory_space=pltpu.VMEM)
ANY = pl.BlockSpec(memory_space=pl.ANY)
HBM = pl.BlockSpec(memory_space=pltpu.HBM)
SMEM = pl.BlockSpec(memory_space=pltpu.SMEM)


def span(s):
    return s.stop - s.start


def dot(a, b, ca, cb):
    return lax.dot_general(a, b, (((ca,), (cb,)), ((), ())), preferred_element_type=F32)


def tap_offset(b):
    return LEFT - HALO + STEP * b


def span(s):
    return s.stop - s.start


def side_targets(owners, neighbour, code, position):
    targets = []
    for s in range(4):
        offset = lax.rem(neighbour[0, s] - position + 1 + owners, owners)
        first = (offset == 0) == (lax.rem(position, 2) == 1)
        source = jnp.where(offset == 1, 0, jnp.where(first, 1, 2))
        edge = code[0, s] & 3
        flipped = (code[0, s] >> 2) & 1
        along = jnp.where(edge < 2, 1, N)
        across = jnp.where(edge < 2, N, 1)
        far = edge & 1
        base = source * (N * N) + flipped * (N - 1) * along + far * (N - 1) * across
        step_k = across * (1 - 2 * far)
        step_m = along * (1 - 2 * flipped)
        n = HALO * N if s < 2 else LEFT * N
        rho = lax.broadcasted_iota(jnp.int32, (n, 1), 0)
        if s < 2:
            m = rho & (N - 1)
            k = rho >> 4
            if s == 0:
                k = HALO - 1 - k
            targets.append(base + step_k * k + step_m * m)
        else:
            m = rho >> 3
            q = rho & (LEFT - 1)
            k = LEFT - 1 - q if s == 2 else q
            targets.append(jnp.where(k < HALO, base + step_k * k + step_m * m, -1))
    return jnp.concatenate(targets, 0)


def prepare_kernel(
    owners, neighbour, code, position, own_hbm, cot_hbm, taps_hbm, win_hbm, wout_hbm,
    onehot, frame, d_hidden, cot_ref, taps_ref, win_ref, own_ref, wout_ref, sems,
):
    copies = [
        pltpu.make_async_copy(src, dst, sems.at[n])
        for n, (src, dst) in enumerate(
            (
                (own_hbm, own_ref),
                (cot_hbm, cot_ref),
                (wout_hbm, wout_ref),
                (win_hbm, win_ref),
                (taps_hbm, taps_ref),
            )
        )
    ]
    for copy in copies:
        copy.start()
    target = side_targets(owners, neighbour, code, position[0])
    lane = lax.broadcasted_iota(jnp.int32, (SIDE_CELLS, 3 * N * N), 1)
    onehot[...] = jnp.where(target == lane, 1.0, 0.0).astype(BF16)
    corner = jnp.zeros((HALO, LEFT, LANES), F32)
    copies[0].wait()
    own = own_ref[...]
    rims = dot(onehot[:, : N * N], own, 1, 0)
    inner = own.astype(F32).reshape(N, N, C)
    for l in range(C // LANES):
        lanes = slice(l * LANES, (l + 1) * LANES)
        for top in (0, HALO + N):
            for left in (0, LEFT + N):
                frame[l, top : top + HALO, left : left + LEFT, :] = corner
        for rows, cols, cells in RIMS:
            frame[l, rows, cols, :] = rims[cells, lanes].reshape(span(rows), span(cols), LANES)
        frame[l, HALO : HALO + N, LEFT : LEFT + N, :] = inner[:, :, lanes]
    copies[1].wait()
    copies[2].wait()
    d_hidden[...] = dot(cot_ref[...], wout_ref[...], 1, 1)
    copies[3].wait()
    copies[4].wait()


def add_rims(cells_to, tile_ref, onehot, frame):
    rims = dot(onehot[:, cells_to], tile_ref[...], 1, 0)
    for l in range(C // LANES):
        lanes = slice(l * LANES, (l + 1) * LANES)
        for rows, cols, cells in RIMS:
            frame[l, rows, cols, :] += rims[cells, lanes].reshape(span(rows), span(cols), LANES)


def one_kernel(start_ref, one_ref, onehot, frame):
    del start_ref
    add_rims(slice(N * N, 2 * N * N), one_ref, onehot, frame)


def forward_kernel(
    core, start_ref, two_ref, onehot, d_hidden_ref, cot_ref, taps_ref, win_ref,
    send_ref, keep_ref, dconv_ref, frame, conv,
):
    del start_ref
    add_rims(slice(2 * N * N, 3 * N * N), two_ref, onehot, frame)
    for l in range(C // LANES):
        lanes = slice(l * LANES, (l + 1) * LANES)
        acc = [None] * N
        for b in range(TAPS):
            off = tap_offset(b)
            coef = [taps_ref[a * TAPS + b : a * TAPS + b + 1, lanes] for a in range(TAPS)]
            for r in range(ROWS):
                x = frame[l, r, off : off + N, :]
                for a in range(TAPS):
                    i = r - STEP * a
                    if 0 <= i < N:
                        term = x * coef[a]
                        acc[i] = term if acc[i] is None else acc[i] + term
        for i in range(N):
            conv[i * N : (i + 1) * N, lanes] = acc[i]
    value = conv[...]
    centred = value - jnp.mean(value, -1, keepdims=True)
    inv_std = lax.rsqrt(jnp.mean(centred * centred, -1, keepdims=True) + 1e-06)
    normed_f = centred * inv_std
    normed = normed_f.astype(BF16)
    cot = cot_ref[...]
    first = core[0] == 0
    d_normed = None
    for h in range(GROUP):
        cols = slice(h * C, (h + 1) * C)
        w_in = win_ref[:, cols]
        pre = dot(normed, w_in, 1, 0)
        square = pre * pre
        t = jnp.tanh(pre * (GELU_A + (GELU_A * GELU_B) * square))
        half = 0.5 + 0.5 * t
        hidden = (pre * half).astype(BF16)
        slope = half + (0.5 * pre) * (1.0 - t * t) * (GELU_A + (3.0 * GELU_A * GELU_B) * square)
        d_pre = (d_hidden_ref[:, cols] * slope).astype(BF16)
        part_out = dot(hidden, cot, 0, 0).astype(BF16)
        part_in = dot(normed, d_pre, 0, 0).astype(BF16)
        send_ref[h] = jnp.where(first, part_out, part_in)
        keep_ref[h] = jnp.where(first, part_in, part_out)
        back = dot(d_pre, w_in, 1, 1)
        d_normed = back if d_normed is None else d_normed + back
    dconv_ref[...] = inv_std * (
        d_normed
        - jnp.mean(d_normed, -1, keepdims=True)
        - normed_f * jnp.mean(d_normed * normed_f, -1, keepdims=True)
    )


def tap_sums(frame, dconv_ref, out_ref):
    out_ref[...] = jnp.zeros(out_ref.shape, F32)
    for l in range(C // LANES):
        lanes = slice(l * LANES, (l + 1) * LANES)
        grad = [dconv_ref[i * N : (i + 1) * N, lanes] for i in range(N)]
        for b in range(TAPS):
            off = tap_offset(b)
            acc = [None] * TAPS
            for r in range(ROWS):
                x = frame[l, r, off : off + N, :]
                for a in range(TAPS):
                    i = r - STEP * a
                    if 0 <= i < N:
                        term = x * grad[i]
                        acc[a] = term if acc[a] is None else acc[a] + term
            for a in range(TAPS):
                t = a * TAPS + b
                out_ref[t // EXTRA, t % EXTRA : t % EXTRA + 1, lanes] = jnp.sum(
                    acc[a], 0, keepdims=True
                )


def backward_kernel(
    frame, onehot, dconv_ref, taps_ref, cot_hbm, _, sums_ref, own_ref, one_ref, two_ref, keep_ref,
    shifted, rim, cot_ref, sem,
):
    del keep_ref
    copy = pltpu.make_async_copy(cot_hbm, cot_ref, sem)
    copy.start()
    tap_sums(frame, dconv_ref, sums_ref)
    residues = (2, 4, 6, 0)
    pad = jnp.zeros((ROWS, 8, LANES), F32)
    for l in range(C // LANES):
        lanes = slice(l * LANES, (l + 1) * LANES)
        grad = [
            [dconv_ref[i * N + 8 * t : i * N + 8 * t + 8, lanes] for t in range(2)]
            for i in range(N)
        ]
        for n, s in enumerate(residues):
            shifted[l, n, :, 0:8, :] = pad
            shifted[l, n, :, 32:40, :] = pad
            pieces = [(b, tap_offset(b) // 8) for b in range(TAPS) if tap_offset(b) % 8 == s]
            coef = {
                (a, b): taps_ref[a * TAPS + b : a * TAPS + b + 1, lanes]
                for a in range(TAPS)
                for b, _ in pieces
            }
            for r in range(ROWS):
                acc = [None] * 3
                for a in range(TAPS):
                    i = r - STEP * a
                    if 0 <= i < N:
                        for b, up in pieces:
                            for t in range(2):
                                term = grad[i][t] * coef[a, b]
                                acc[t + up] = term if acc[t + up] is None else acc[t + up] + term
                for t in range(3):
                    shifted[l, n, r, 8 + 8 * t : 16 + 8 * t, :] = (
                        jnp.zeros((8, LANES), F32) if acc[t] is None else acc[t]
                    )

        def gather(rows, first_col, count):
            total = None
            for n, s in enumerate(residues):
                at = 8 + first_col - s
                piece = shifted[l, n, rows, at : at + count, :]
                total = piece if total is None else total + piece
            return total

        top = gather(slice(0, HALO), LEFT, N)
        bottom = gather(slice(HALO + N, ROWS), LEFT, N)
        middle = slice(HALO, HALO + N)
        left = gather(middle, 0, 8)
        right = gather(middle, LEFT + N, 8)
        inner = gather(middle, LEFT, N)
        at = 0
        for block in (top, bottom, left, right):
            n = block.shape[0] * block.shape[1]
            rim[at : at + n, lanes] = block.reshape(n, LANES).astype(BF16)
            at += n
        own_ref[:, lanes] = inner.reshape(N * N, LANES)
    copy.wait()
    cells = rim[...]
    own_ref[...] += cot_ref[...].astype(F32) + dot(onehot[:, : N * N], cells, 0, 0)
    one_ref[...] = dot(onehot[:, N * N : 2 * N * N], cells, 0, 0).astype(BF16)
    two_ref[...] = dot(onehot[:, 2 * N * N :], cells, 0, 0).astype(BF16)


def spread_kernel(place, keep_ref, got_ref, taps_ref, own_ref, one_ref, two_ref, three_ref):
    for d, out in enumerate((own_ref, one_ref, two_ref, three_ref)):
        j = place[0] ^ d
        out[:C, :] = (keep_ref[j].astype(F32) + got_ref[j].astype(F32)).astype(out.dtype)
        out[C:, :] = taps_ref[j].astype(out.dtype)


def store_kernel(scale, picks, given, last, core, mine_at, theirs_at, *refs):
    count = len(picks) + (2 * GROUP if last else 0)
    blocks, taps = refs[: len(picks)], refs[len(picks) : count]
    refs = refs[count + given :]
    in_hbm, out_hbm = refs[:2]
    copies = []
    if last:
        kernel_hbm, stage, sems, rows, kernel_ref = refs[2:]
        for n, block in enumerate(taps):
            at = (mine_at if n < GROUP else theirs_at)[0] ^ (n % GROUP)
            rows[n // GROUP, at] = block[C:, :].astype(F32)
        for j in range(GROUP):
            n = min(EXTRA, TAPS * TAPS - j * EXTRA)
            kernel_ref[j * EXTRA : j * EXTRA + n, :] = (rows[0, j, :n, :] + rows[1, j, :n, :]) * scale
        copies.append(pltpu.make_async_copy(kernel_ref, kernel_hbm, sems.at[GROUP]))
        copies[0].start()
    else:
        stage, sems = refs[2:]
    first = core[0] == 0
    pairs = []
    for n, (half, d) in enumerate(picks):
        stage[n] = blocks[n][:C, :].astype(F32) * scale
        at = pl.ds(pl.multiple_of(((theirs_at if half else mine_at)[0] ^ d) * C, C), C)
        into_in = pltpu.make_async_copy(stage.at[n], in_hbm.at[:, at], sems.at[n])
        into_out = pltpu.make_async_copy(stage.at[n], out_hbm.at[at, :], sems.at[n])
        to_in = jnp.logical_not(first) if half else first
        pl.when(to_in)(into_in.start)
        pl.when(jnp.logical_not(to_in))(into_out.start)
        pairs.append((to_in, into_in, into_out))
    for copy in copies:
        copy.wait()
    for to_in, into_in, into_out in pairs:
        pl.when(to_in)(into_in.wait)
        pl.when(jnp.logical_not(to_in))(into_out.wait)


def join_kernel(own_ref, one_ref, two_ref, out_ref):
    out_ref[...] = (own_ref[...] + one_ref[...].astype(F32) + two_ref[...].astype(F32)).astype(BF16)


def in_hbm(x):
    return pltpu.with_memory_space_constraint(x, pltpu.HBM)


def call(kernel, outs, scratch=(), specs=(), flops=700_000_000, aliases={}, out_specs=None, vmem=16):
    return pl.pallas_call(
        kernel,
        out_shape=outs,
        in_specs=specs,
        out_specs=out_specs or jax.tree.map(lambda _: VMEM, outs),
        scratch_shapes=scratch,
        input_output_aliases=aliases,
        compiler_params=pltpu.CompilerParams(vmem_limit_bytes=vmem * 1024 * 1024),
        cost_estimate=pl.CostEstimate(flops=flops, bytes_accessed=4_000_000, transcendentals=0),
    )


def body(features, cotangent, kernel, weight_in, weight_out, tile_neighbour, edge_code):
    owners = lax.axis_size("tile")
    members = lax.axis_size("ens")
    position = lax.axis_index("tile")
    member = lax.axis_index("ens")
    devices = owners * members
    scale = 1.0 / math.sqrt(devices * N * N)
    both = ("tile", "ens")
    struct = jax.ShapeDtypeStruct

    def one_over(x):
        return lax.ppermute(x, "tile", [(i, i ^ 1) for i in range(owners)])

    def two_over(x):
        moves = [(i, (i + 1 if i % 2 else i - 1) % owners) for i in range(owners)]
        return lax.ppermute(x, "tile", moves)

    index = position * members + member
    free = [1 << n for n in range(2, members.bit_length() - 1)]
    free += [members << n for n in range(1, owners.bit_length() - 1)]
    pairs = ((2, members), (free[0], free[1]))
    later = [tuple(free[n : n + 2]) for n in range(2, len(free), 2)]

    def swap(x, even, odd):
        return lax.ppermute(x, both, [(i, i ^ (odd if i % 2 else even)) for i in range(devices)])

    def digit(pair):
        return jnp.where(index & pair[0], 1, 0) + jnp.where(index & pair[1], 2, 0)

    core = member % 2
    digits = (digit(pairs[0]), digit(pairs[1]))
    mine_at = jnp.where(core == 0, digits[0], digits[1]).astype(jnp.int32).reshape(1)
    theirs_at = jnp.where(core == 0, digits[1], digits[0]).astype(jnp.int32).reshape(1)
    core = core.reshape(1).astype(jnp.int32)
    combos = [[p[0], p[1], p[0] + p[1]] for p in pairs]

    own = features.reshape(N * N, C)
    cot_rows = cotangent.reshape(N * N, C)
    one = one_over(own)
    two = two_over(own)

    frame = pltpu.VMEM((2, ROWS, FRAME, LANES), F32)
    onehot, frame_one, d_hidden, cot, taps, w_in = call(
        functools.partial(prepare_kernel, owners),
        (
            pltpu.VMEM((SIDE_CELLS, 3 * N * N), BF16),
            frame,
            pltpu.VMEM((N * N, HID), F32),
            pltpu.VMEM((N * N, C), BF16),
            pltpu.VMEM((TAPS * TAPS, C), F32),
            pltpu.VMEM((C, HID), BF16),
        ),
        [
            pltpu.VMEM((N * N, C), BF16),
            pltpu.VMEM((HID, C), BF16),
            pltpu.SemaphoreType.DMA((5,)),
        ],
        [SMEM] * 3 + [HBM] * 5,
    )(
        tile_neighbour, edge_code, position.reshape(1).astype(jnp.int32),
        *map(in_hbm, (own, cot_rows, kernel, weight_in, weight_out)),
    )
    frame_one = call(
        one_kernel, frame, (), [VMEM] * 3, aliases={0: 0}
    )(frame_one, one, onehot)
    half = pltpu.VMEM((GROUP, C, C), BF16)
    send, keep, dconv, frame_two = call(
        forward_kernel,
        (half, half, pltpu.VMEM((N * N, C), F32), frame),
        [pltpu.VMEM((N * N, C), F32)],
        [SMEM] + [VMEM] * 7,
        flops=1_000_000_000,
        aliases={1: 3},
    )(core, frame_one, two, onehot, d_hidden, cot, taps, w_in)
    got = swap(send, 1, 1)
    part_taps, grad_own, grad_one, grad_two, keep = call(
        backward_kernel,
        (
            pltpu.VMEM((GROUP, EXTRA, C), F32),
            pltpu.VMEM((N * N, C), F32),
            pltpu.VMEM((N * N, C), BF16),
            pltpu.VMEM((N * N, C), BF16),
            half,
        ),
        [
            pltpu.VMEM((2, 4, ROWS, 40, LANES), F32),
            pltpu.VMEM((SIDE_CELLS, C), BF16),
            pltpu.VMEM((N * N, C), BF16),
            pltpu.SemaphoreType.DMA,
        ],
        [VMEM] * 4 + [HBM, VMEM],
        aliases={5: 4},
    )(frame_two, onehot, dconv, taps, in_hbm(cot_rows), keep)

    block = struct((C + EXTRA, C), BF16)
    pieces = call(
        spread_kernel, (block,) * GROUP, (), [SMEM] + [VMEM] * 3
    )(mine_at, keep, got, part_taps)
    total = pieces[0].astype(F32)
    for piece, even, odd in reversed(list(zip(pieces[1:], *combos))):
        total = total + swap(piece, even, odd).astype(F32)
    total = total.astype(BF16)

    back_two = two_over(grad_two)
    back_one = one_over(grad_one)
    for even, odd in [(pairs[1], pairs[0])] + [(p, p) for p in later]:
        got = [swap(total, a, b) for a, b in zip(even, odd)]
        summed = total.astype(F32) + got[0].astype(F32)
        if len(got) == 2:
            third = swap(total, sum(even), sum(odd))
            summed = summed + (got[1].astype(F32) + third.astype(F32))
        total = summed.astype(BF16)
    grad_features = call(
        join_kernel, struct((N * N, C), BF16), (), [VMEM] * 3, flops=JOIN_COST
    )(grad_own, back_one, back_two)
    total, grad_features = lax.optimization_barrier((total, grad_features))
    mine = [total] + [swap(total, even, odd) for even, odd in zip(*combos)]
    theirs = [swap(x, 1, 1) for x in mine]
    grads = (struct((C, HID), F32), struct((HID, C), F32))
    stage = [pltpu.VMEM((GROUP, C, C), F32), pltpu.SemaphoreType.DMA((GROUP + 1,))]
    halves = (mine, theirs)

    def store(picks, given, last=False):
        blocks = [halves[half][d] for half, d in picks] + ([*mine, *theirs] if last else [])
        count = 3 + len(blocks)
        return call(
            functools.partial(store_kernel, scale, picks, len(given), last),
            (*grads, struct((TAPS * TAPS, C), F32)) if last else grads,
            stage
            + (
                [pltpu.VMEM((2, GROUP, EXTRA, C), F32), pltpu.VMEM((TAPS * TAPS, C), F32)]
                if last
                else []
            ),
            [SMEM] * 3 + [VMEM] * len(blocks) + [ANY] * len(given),
            out_specs=(ANY,) * (3 if last else 2),
            aliases={count + n: n for n in range(len(given))},
        )(core, mine_at, theirs_at, *blocks, *given)

    given = store([(0, d) for d in range(GROUP)], ())
    grad_in, grad_out, grad_kernel = store([(1, d) for d in range(GROUP)], given, True)
    return grad_features.reshape(features.shape), grad_kernel, grad_in, grad_out


def solution(mesh):
    halved = P("ens", "tile", None, None, None)
    in_specs = (halved, halved, P(), P(), P(), P("tile", None), P("tile", None))
    out_specs = (halved, P(), P(), P())
    return jax.shard_map(body, mesh=mesh, in_specs=in_specs, out_specs=out_specs, check_vma=False)
```

```python
import functools
import math

import jax
import jax.numpy as jnp
from jax import lax
from jax.experimental import pallas as pl
from jax.experimental.pallas import tpu as pltpu
from jax.sharding import PartitionSpec as P

C = 256
HID = 1024
TAPS = 7
STEP = 2
HALO = 6
N = 16
ROWS = N + 2 * HALO
LANES = 128
FRAME = 32
LEFT = 8
GROUP = 4
STARTS = ((3, 2, 1), (3, 2, 1), (3, 2, 1))
JOIN_COST = 30_000_000_000
EXTRA = 16
F32 = jnp.float32
BF16 = jnp.bfloat16
GELU_A = math.sqrt(2.0 / math.pi)
GELU_B = 0.044715
SIDE_CELLS = 2 * HALO * N + 2 * LEFT * N
RIMS = (
    (slice(0, HALO), slice(LEFT, LEFT + N), slice(0, 96)),
    (slice(HALO + N, ROWS), slice(LEFT, LEFT + N), slice(96, 192)),
    (slice(HALO, HALO + N), slice(0, LEFT), slice(192, 320)),
    (slice(HALO, HALO + N), slice(LEFT + N, FRAME), slice(320, 448)),
)
VMEM = pl.BlockSpec(memory_space=pltpu.VMEM)
ANY = pl.BlockSpec(memory_space=pl.ANY)
HBM = pl.BlockSpec(memory_space=pltpu.HBM)
SMEM = pl.BlockSpec(memory_space=pltpu.SMEM)


def span(s):
    return s.stop - s.start


def dot(a, b, ca, cb):
    return lax.dot_general(a, b, (((ca,), (cb,)), ((), ())), preferred_element_type=F32)


def tap_offset(b):
    return LEFT - HALO + STEP * b


def span(s):
    return s.stop - s.start


def side_targets(owners, neighbour, code, position):
    targets = []
    for s in range(4):
        offset = lax.rem(neighbour[0, s] - position + 1 + owners, owners)
        first = (offset == 0) == (lax.rem(position, 2) == 1)
        source = jnp.where(offset == 1, 0, jnp.where(first, 1, 2))
        edge = code[0, s] & 3
        flipped = (code[0, s] >> 2) & 1
        along = jnp.where(edge < 2, 1, N)
        across = jnp.where(edge < 2, N, 1)
        far = edge & 1
        base = source * (N * N) + flipped * (N - 1) * along + far * (N - 1) * across
        step_k = across * (1 - 2 * far)
        step_m = along * (1 - 2 * flipped)
        n = HALO * N if s < 2 else LEFT * N
        rho = lax.broadcasted_iota(jnp.int32, (n, 1), 0)
        if s < 2:
            m = rho & (N - 1)
            k = rho >> 4
            if s == 0:
                k = HALO - 1 - k
            targets.append(base + step_k * k + step_m * m)
        else:
            m = rho >> 3
            q = rho & (LEFT - 1)
            k = LEFT - 1 - q if s == 2 else q
            targets.append(jnp.where(k < HALO, base + step_k * k + step_m * m, -1))
    return jnp.concatenate(targets, 0)


def prepare_kernel(
    owners, position, neighbour_hbm, code_hbm, own_hbm, taps_hbm, cot_hbm, wout_hbm, win_hbm,
    onehot, frame, conv, d_hidden, cot_ref, taps_ref, win_ref,
    neighbour, code, own_ref, wout_ref, sems,
):
    copies = [
        pltpu.make_async_copy(src, dst, sems.at[n])
        for n, (src, dst) in enumerate(
            (
                (neighbour_hbm, neighbour),
                (code_hbm, code),
                (own_hbm, own_ref),
                (taps_hbm, taps_ref),
                (cot_hbm, cot_ref),
                (wout_hbm, wout_ref),
                (win_hbm, win_ref),
            )
        )
    ]
    for copy in copies:
        copy.start()
    copies[0].wait()
    copies[1].wait()
    target = side_targets(owners, neighbour, code, position[0])
    lane = lax.broadcasted_iota(jnp.int32, (SIDE_CELLS, 3 * N * N), 1)
    onehot[...] = jnp.where(target == lane, 1.0, 0.0).astype(BF16)
    corner = jnp.zeros((HALO, LEFT, LANES), F32)
    copies[2].wait()
    own = own_ref[...]
    rims = dot(onehot[:, : N * N], own, 1, 0)
    inner = own.astype(F32).reshape(N, N, C)
    for l in range(C // LANES):
        lanes = slice(l * LANES, (l + 1) * LANES)
        for top in (0, HALO + N):
            for left in (0, LEFT + N):
                frame[l, top : top + HALO, left : left + LEFT, :] = corner
        for rows, cols, cells in RIMS:
            frame[l, rows, cols, :] = rims[cells, lanes].reshape(span(rows), span(cols), LANES)
        frame[l, HALO : HALO + N, LEFT : LEFT + N, :] = inner[:, :, lanes]
    copies[3].wait()
    for l in range(C // LANES):
        lanes = slice(l * LANES, (l + 1) * LANES)
        acc = [None] * N
        for b in range(TAPS):
            off = tap_offset(b)
            coef = [taps_ref[a * TAPS + b : a * TAPS + b + 1, lanes] for a in range(TAPS)]
            for r in range(ROWS):
                x = frame[l, r, off : off + N, :]
                for a in range(TAPS):
                    i = r - STEP * a
                    if 0 <= i < N:
                        term = x * coef[a]
                        acc[i] = term if acc[i] is None else acc[i] + term
        for i in range(N):
            conv[i * N : (i + 1) * N, lanes] = acc[i]
    copies[4].wait()
    copies[5].wait()
    d_hidden[...] = dot(cot_ref[...], wout_ref[...], 1, 1)
    copies[6].wait()


def one_kernel(one_ref, onehot, rims):
    rims[...] = dot(onehot[:, N * N : 2 * N * N], one_ref[...], 1, 0)


def add_rims(rims_ref, two_ref, onehot, taps_ref, frame, conv, alone):
    rims = rims_ref[...] + dot(onehot[:, 2 * N * N :], two_ref[...], 1, 0)
    alone[...] = jnp.zeros(alone.shape, F32)
    for l in range(C // LANES):
        lanes = slice(l * LANES, (l + 1) * LANES)
        for rows, cols, cells in RIMS:
            block = rims[cells, lanes].reshape(span(rows), span(cols), LANES)
            frame[l, rows, cols, :] += block
            alone[l, rows, cols, :] = block
    for l in range(C // LANES):
        lanes = slice(l * LANES, (l + 1) * LANES)
        acc = [[conv[i * N + 8 * t : i * N + 8 * t + 8, lanes] for t in range(2)] for i in range(N)]
        for b in range(TAPS):
            off = tap_offset(b)
            coef = [taps_ref[a * TAPS + b : a * TAPS + b + 1, lanes] for a in range(TAPS)]
            for r in range(ROWS):
                middle = HALO <= r < HALO + N
                for t in range(2):
                    start = off + 8 * t
                    if middle and start >= LEFT and start + 8 <= LEFT + N:
                        continue
                    x = alone[l, r, start : start + 8, :]
                    for a in range(TAPS):
                        i = r - STEP * a
                        if 0 <= i < N:
                            acc[i][t] = acc[i][t] + x * coef[a]
        for i in range(N):
            for t in range(2):
                conv[i * N + 8 * t : i * N + 8 * t + 8, lanes] = acc[i][t]


def forward_kernel(
    core, frame_in, conv_in, rims_ref, two_ref, onehot, d_hidden_ref, cot_ref, taps_ref, win_ref,
    send_ref, keep_ref, dconv_ref, frame, conv, alone,
):
    del frame_in, conv_in
    add_rims(rims_ref, two_ref, onehot, taps_ref, frame, conv, alone)
    value = conv[...]
    centred = value - jnp.mean(value, -1, keepdims=True)
    inv_std = lax.rsqrt(jnp.mean(centred * centred, -1, keepdims=True) + 1e-06)
    normed_f = centred * inv_std
    normed = normed_f.astype(BF16)
    cot = cot_ref[...]
    first = core[0] == 0
    d_normed = None
    for h in range(GROUP):
        cols = slice(h * C, (h + 1) * C)
        w_in = win_ref[:, cols]
        pre = dot(normed, w_in, 1, 0)
        square = pre * pre
        t = jnp.tanh(pre * (GELU_A + (GELU_A * GELU_B) * square))
        half = 0.5 + 0.5 * t
        value = pre * half
        hidden = value.astype(BF16)
        slope = half + value * ((1.0 - t) * (GELU_A + (3.0 * GELU_A * GELU_B) * square))
        d_pre = (d_hidden_ref[:, cols] * slope).astype(BF16)
        part_out = dot(hidden, cot, 0, 0).astype(BF16)
        part_in = dot(normed, d_pre, 0, 0).astype(BF16)
        send_ref[h] = jnp.where(first, part_out, part_in)
        keep_ref[h] = jnp.where(first, part_in, part_out)
        back = dot(d_pre, w_in, 1, 1)
        d_normed = back if d_normed is None else d_normed + back
    dconv_ref[...] = inv_std * (
        d_normed
        - jnp.mean(d_normed, -1, keepdims=True)
        - normed_f * jnp.mean(d_normed * normed_f, -1, keepdims=True)
    )


def tap_sums(frame, dconv_ref, out_ref):
    out_ref[...] = jnp.zeros(out_ref.shape, F32)
    for l in range(C // LANES):
        lanes = slice(l * LANES, (l + 1) * LANES)
        grad = [dconv_ref[i * N : (i + 1) * N, lanes] for i in range(N)]
        for b in range(TAPS):
            off = tap_offset(b)
            acc = [None] * TAPS
            for r in range(ROWS):
                x = frame[l, r, off : off + N, :]
                for a in range(TAPS):
                    i = r - STEP * a
                    if 0 <= i < N:
                        term = x * grad[i]
                        acc[a] = term if acc[a] is None else acc[a] + term
            for a in range(TAPS):
                t = a * TAPS + b
                out_ref[t // EXTRA, t % EXTRA : t % EXTRA + 1, lanes] = jnp.sum(
                    acc[a], 0, keepdims=True
                )


def tap_kernel(frame, dconv_in, keep_in, sums_ref, dconv_ref, keep_ref):
    del dconv_in, keep_in, keep_ref
    tap_sums(frame, dconv_ref, sums_ref)


def backward_kernel(
    onehot, dconv_ref, taps_ref, cot_hbm, own_ref, one_ref, two_ref, shifted, rim, cot_ref, sem,
):
    copy = pltpu.make_async_copy(cot_hbm, cot_ref, sem)
    copy.start()
    residues = (2, 4, 6, 0)
    pad = jnp.zeros((ROWS, 8, LANES), F32)
    for l in range(C // LANES):
        lanes = slice(l * LANES, (l + 1) * LANES)
        grad = [
            [dconv_ref[i * N + 8 * t : i * N + 8 * t + 8, lanes] for t in range(2)]
            for i in range(N)
        ]
        for n, s in enumerate(residues):
            shifted[l, n, :, 0:8, :] = pad
            shifted[l, n, :, 32:40, :] = pad
            pieces = [(b, tap_offset(b) // 8) for b in range(TAPS) if tap_offset(b) % 8 == s]
            coef = {
                (a, b): taps_ref[a * TAPS + b : a * TAPS + b + 1, lanes]
                for a in range(TAPS)
                for b, _ in pieces
            }
            for r in range(ROWS):
                acc = [None] * 3
                for a in range(TAPS):
                    i = r - STEP * a
                    if 0 <= i < N:
                        for b, up in pieces:
                            for t in range(2):
                                term = grad[i][t] * coef[a, b]
                                acc[t + up] = term if acc[t + up] is None else acc[t + up] + term
                for t in range(3):
                    shifted[l, n, r, 8 + 8 * t : 16 + 8 * t, :] = (
                        jnp.zeros((8, LANES), F32) if acc[t] is None else acc[t]
                    )

        def gather(rows, first_col, count):
            total = None
            for n, s in enumerate(residues):
                at = 8 + first_col - s
                piece = shifted[l, n, rows, at : at + count, :]
                total = piece if total is None else total + piece
            return total

        top = gather(slice(0, HALO), LEFT, N)
        bottom = gather(slice(HALO + N, ROWS), LEFT, N)
        middle = slice(HALO, HALO + N)
        left = gather(middle, 0, 8)
        right = gather(middle, LEFT + N, 8)
        inner = gather(middle, LEFT, N)
        at = 0
        for block in (top, bottom, left, right):
            n = block.shape[0] * block.shape[1]
            rim[at : at + n, lanes] = block.reshape(n, LANES).astype(BF16)
            at += n
        own_ref[:, lanes] = inner.reshape(N * N, LANES)
    copy.wait()
    cells = rim[...]
    own_ref[...] += cot_ref[...].astype(F32) + dot(onehot[:, : N * N], cells, 0, 0)
    one_ref[...] = dot(onehot[:, N * N : 2 * N * N], cells, 0, 0).astype(BF16)
    two_ref[...] = dot(onehot[:, 2 * N * N :], cells, 0, 0).astype(BF16)


def spread_kernel(place, keep_ref, got_ref, taps_ref, own_ref, one_ref, two_ref, three_ref):
    for d, out in enumerate((own_ref, one_ref, two_ref, three_ref)):
        j = place[0] ^ d
        out[:C, :] = (keep_ref[j].astype(F32) + got_ref[j].astype(F32)).astype(out.dtype)
        out[C:, :] = taps_ref[j].astype(out.dtype)


def store_kernel(scale, picks, given, last, core, mine_at, theirs_at, *refs):
    count = len(picks) + (2 * GROUP if last else 0)
    blocks, taps = refs[: len(picks)], refs[len(picks) : count]
    refs = refs[count + given :]
    in_hbm, out_hbm = refs[:2]
    copies = []
    if last:
        kernel_hbm, stage, sems, rows, kernel_ref = refs[2:]
        for n, block in enumerate(taps):
            at = (mine_at if n < GROUP else theirs_at)[0] ^ (n % GROUP)
            rows[n // GROUP, at] = block[C:, :].astype(F32)
        for j in range(GROUP):
            n = min(EXTRA, TAPS * TAPS - j * EXTRA)
            kernel_ref[j * EXTRA : j * EXTRA + n, :] = (rows[0, j, :n, :] + rows[1, j, :n, :]) * scale
        copies.append(pltpu.make_async_copy(kernel_ref, kernel_hbm, sems.at[GROUP]))
        copies[0].start()
    else:
        stage, sems = refs[2:]
    first = core[0] == 0
    pairs = []
    for n, (half, d) in enumerate(picks):
        stage[n] = blocks[n][:C, :].astype(F32) * scale
        at = pl.ds(pl.multiple_of(((theirs_at if half else mine_at)[0] ^ d) * C, C), C)
        into_in = pltpu.make_async_copy(stage.at[n], in_hbm.at[:, at], sems.at[n])
        into_out = pltpu.make_async_copy(stage.at[n], out_hbm.at[at, :], sems.at[n])
        to_in = jnp.logical_not(first) if half else first
        pl.when(to_in)(into_in.start)
        pl.when(jnp.logical_not(to_in))(into_out.start)
        pairs.append((to_in, into_in, into_out))
    for copy in copies:
        copy.wait()
    for to_in, into_in, into_out in pairs:
        pl.when(to_in)(into_in.wait)
        pl.when(jnp.logical_not(to_in))(into_out.wait)


def join_kernel(own_ref, other_ref, out_ref):
    out_ref[...] = (own_ref[...] + other_ref[...].astype(F32)).astype(out_ref.dtype)


def in_hbm(x):
    return pltpu.with_memory_space_constraint(x, pltpu.HBM)


def in_vmem(x):
    return pltpu.with_memory_space_constraint(x, pltpu.VMEM)


def call(kernel, outs, scratch=(), specs=(), flops=300_000_000, aliases={}, out_specs=None, vmem=16):
    return pl.pallas_call(
        kernel,
        out_shape=outs,
        in_specs=specs,
        out_specs=out_specs or jax.tree.map(lambda _: VMEM, outs),
        scratch_shapes=scratch,
        input_output_aliases=aliases,
        compiler_params=pltpu.CompilerParams(vmem_limit_bytes=vmem * 1024 * 1024),
        cost_estimate=pl.CostEstimate(flops=flops, bytes_accessed=4_000_000, transcendentals=0),
    )


def body(features, cotangent, kernel, weight_in, weight_out, tile_neighbour, edge_code):
    owners = lax.axis_size("tile")
    members = lax.axis_size("ens")
    position = lax.axis_index("tile")
    member = lax.axis_index("ens")
    devices = owners * members
    scale = 1.0 / math.sqrt(devices * N * N)
    both = ("tile", "ens")
    struct = jax.ShapeDtypeStruct

    def one_over(x):
        return lax.ppermute(x, "tile", [(i, i ^ 1) for i in range(owners)])

    def two_over(x):
        moves = [(i, (i + 1 if i % 2 else i - 1) % owners) for i in range(owners)]
        return lax.ppermute(x, "tile", moves)

    index = position * members + member
    free = [1 << n for n in range(2, members.bit_length() - 1)]
    free += [members << n for n in range(1, owners.bit_length() - 1)]
    pairs = ((2, members), (free[0], free[1]))
    later = [tuple(free[n : n + 2]) for n in range(2, len(free), 2)]

    def swap(x, even, odd):
        return lax.ppermute(x, both, [(i, i ^ (odd if i % 2 else even)) for i in range(devices)])

    def digit(pair):
        return jnp.where(index & pair[0], 1, 0) + jnp.where(index & pair[1], 2, 0)

    core = member % 2
    digits = (digit(pairs[0]), digit(pairs[1]))
    mine_at = jnp.where(core == 0, digits[0], digits[1]).astype(jnp.int32).reshape(1)
    theirs_at = jnp.where(core == 0, digits[1], digits[0]).astype(jnp.int32).reshape(1)
    core = core.reshape(1).astype(jnp.int32)
    combos = [[p[0], p[1], p[0] + p[1]] for p in pairs]

    own = features.reshape(N * N, C)
    cot_rows = cotangent.reshape(N * N, C)
    one = one_over(own)
    two = two_over(own)

    frame = pltpu.VMEM((2, ROWS, FRAME, LANES), F32)
    cells = pltpu.VMEM((N * N, C), F32)
    onehot, frame_own, conv_own, d_hidden, cot, taps, w_in = call(
        functools.partial(prepare_kernel, owners),
        (
            pltpu.VMEM((SIDE_CELLS, 3 * N * N), BF16),
            frame,
            cells,
            pltpu.VMEM((N * N, HID), F32),
            pltpu.VMEM((N * N, C), BF16),
            pltpu.VMEM((TAPS * TAPS, C), F32),
            pltpu.VMEM((C, HID), BF16),
        ),
        [
            pltpu.SMEM((1, 4), jnp.int32),
            pltpu.SMEM((1, 4), jnp.int32),
            pltpu.VMEM((N * N, C), BF16),
            pltpu.VMEM((HID, C), BF16),
            pltpu.SemaphoreType.DMA((7,)),
        ],
        [SMEM] + [HBM] * 7,
    )(
        position.reshape(1).astype(jnp.int32),
        *map(in_hbm, (tile_neighbour, edge_code, own, kernel, cot_rows, weight_out, weight_in)),
    )
    rims = call(one_kernel, pltpu.VMEM((SIDE_CELLS, C), F32), (), [VMEM] * 2)(one, onehot)
    half = pltpu.VMEM((GROUP, C, C), BF16)
    send, keep, dconv, frame_two, _ = call(
        forward_kernel,
        (half, half, cells, frame, cells),
        [frame],
        [SMEM] + [VMEM] * 9,
        flops=1_000_000_000,
        aliases={1: 3, 2: 4},
    )(core, frame_own, conv_own, rims, two, onehot, d_hidden, cot, taps, w_in)
    got = swap(send, 1, 1)
    part_taps, dconv, keep = call(
        tap_kernel,
        (pltpu.VMEM((GROUP, EXTRA, C), F32), cells, half),
        (),
        [VMEM] * 3,
        aliases={1: 1, 2: 2},
    )(frame_two, dconv, keep)
    block = pltpu.VMEM((C + EXTRA, C), BF16)
    pieces = call(
        spread_kernel, (block,) * GROUP, (), [SMEM] + [VMEM] * 3
    )(mine_at, keep, in_vmem(got), part_taps)
    total = pieces[0].astype(F32)
    for d in STARTS[0]:
        total = total + swap(pieces[d], combos[0][d - 1], combos[1][d - 1]).astype(F32)
    total = total.astype(BF16)

    grad_own, grad_one, grad_two = call(
        backward_kernel,
        (cells, pltpu.VMEM((N * N, C), BF16), pltpu.VMEM((N * N, C), BF16)),
        [
            pltpu.VMEM((2, 4, ROWS, 40, LANES), F32),
            pltpu.VMEM((SIDE_CELLS, C), BF16),
            pltpu.VMEM((N * N, C), BF16),
            pltpu.SemaphoreType.DMA,
        ],
        [VMEM] * 3 + [HBM],
    )(onehot, dconv, taps, in_hbm(cot_rows))
    back_two = two_over(grad_two)
    back_one = one_over(grad_one)
    for even, odd in [(pairs[1], pairs[0])] + [(p, p) for p in later]:
        if len(even) == 2:
            even, odd = (*even, sum(even)), (*odd, sum(odd))
        order = [d for d in reversed(STARTS[1]) if d <= len(even)]
        got = {d: swap(total, even[d - 1], odd[d - 1]).astype(F32) for d in order}
        summed = total.astype(F32) + got[1]
        if len(even) == 3:
            summed = summed + (got[2] + got[3])
        total = summed.astype(BF16)
    joined = call(
        join_kernel, pltpu.VMEM((N * N, C), F32), (), [VMEM] * 2, flops=JOIN_COST
    )(grad_own, back_one)
    total, joined = lax.optimization_barrier((total, joined))
    mine = {d: swap(total, combos[0][d - 1], combos[1][d - 1]) for d in reversed(STARTS[2])}
    mine = [total, mine[1], mine[2], mine[3]]
    grad_features = call(
        join_kernel, struct((N * N, C), BF16), (), [VMEM] * 2, flops=JOIN_COST
    )(joined, back_two)
    mine[0], grad_features = lax.optimization_barrier((mine[0], grad_features))
    theirs = [swap(x, 1, 1) for x in mine]
    grads = (struct((C, HID), F32), struct((HID, C), F32))
    stage = [pltpu.VMEM((GROUP, C, C), F32), pltpu.SemaphoreType.DMA((GROUP + 1,))]
    halves = (mine, theirs)

    def store(picks, given, last=False):
        blocks = [halves[half][d] for half, d in picks] + ([*mine, *theirs] if last else [])
        count = 3 + len(blocks)
        return call(
            functools.partial(store_kernel, scale, picks, len(given), last),
            (*grads, struct((TAPS * TAPS, C), F32)) if last else grads,
            stage
            + (
                [pltpu.VMEM((2, GROUP, EXTRA, C), F32), pltpu.VMEM((TAPS * TAPS, C), F32)]
                if last
                else []
            ),
            [SMEM] * 3 + [VMEM] * len(blocks) + [ANY] * len(given),
            out_specs=(ANY,) * (3 if last else 2),
            aliases={count + n: n for n in range(len(given))},
        )(core, mine_at, theirs_at, *blocks, *given)

    given = store([(0, d) for d in range(GROUP)], ())
    grad_in, grad_out, grad_kernel = store([(1, d) for d in range(GROUP)], given, True)
    return grad_features.reshape(features.shape), grad_kernel, grad_in, grad_out


def solution(mesh):
    halved = P("ens", "tile", None, None, None)
    in_specs = (halved, halved, P(), P(), P(), P("tile", None), P("tile", None))
    out_specs = (halved, P(), P(), P())
    return jax.shard_map(body, mesh=mesh, in_specs=in_specs, out_specs=out_specs, check_vma=False)
```

```python
import functools
import math

import jax
import jax.numpy as jnp
from jax import lax
from jax.experimental import pallas as pl
from jax.experimental.pallas import tpu as pltpu
from jax.sharding import PartitionSpec as P

C = 256
HID = 1024
TAPS = 7
STEP = 2
HALO = 6
N = 16
ROWS = N + 2 * HALO
LANES = 128
FRAME = 32
LEFT = 8
GROUP = 4
STARTS = ((3, 2, 1), (3, 2, 1), (3, 2, 1))
JOIN_COST = 30_000_000_000
EXTRA = 16
F32 = jnp.float32
BF16 = jnp.bfloat16
GELU_A = math.sqrt(2.0 / math.pi)
GELU_B = 0.044715
SIDE_CELLS = 2 * HALO * N + 2 * LEFT * N
RIMS = (
    (slice(0, HALO), slice(LEFT, LEFT + N), slice(0, 96)),
    (slice(HALO + N, ROWS), slice(LEFT, LEFT + N), slice(96, 192)),
    (slice(HALO, HALO + N), slice(0, LEFT), slice(192, 320)),
    (slice(HALO, HALO + N), slice(LEFT + N, FRAME), slice(320, 448)),
)
VMEM = pl.BlockSpec(memory_space=pltpu.VMEM)
ANY = pl.BlockSpec(memory_space=pl.ANY)
HBM = pl.BlockSpec(memory_space=pltpu.HBM)
SMEM = pl.BlockSpec(memory_space=pltpu.SMEM)


def span(s):
    return s.stop - s.start


def dot(a, b, ca, cb):
    return lax.dot_general(a, b, (((ca,), (cb,)), ((), ())), preferred_element_type=F32)


def tap_offset(b):
    return LEFT - HALO + STEP * b


def span(s):
    return s.stop - s.start


def side_targets(owners, neighbour, code, position):
    targets = []
    for s in range(4):
        offset = lax.rem(neighbour[0, s] - position + 1 + owners, owners)
        first = (offset == 0) == (lax.rem(position, 2) == 1)
        source = jnp.where(offset == 1, 0, jnp.where(first, 1, 2))
        edge = code[0, s] & 3
        flipped = (code[0, s] >> 2) & 1
        along = jnp.where(edge < 2, 1, N)
        across = jnp.where(edge < 2, N, 1)
        far = edge & 1
        base = source * (N * N) + flipped * (N - 1) * along + far * (N - 1) * across
        step_k = across * (1 - 2 * far)
        step_m = along * (1 - 2 * flipped)
        n = HALO * N if s < 2 else LEFT * N
        rho = lax.broadcasted_iota(jnp.int32, (n, 1), 0)
        if s < 2:
            m = rho & (N - 1)
            k = rho >> 4
            if s == 0:
                k = HALO - 1 - k
            targets.append(base + step_k * k + step_m * m)
        else:
            m = rho >> 3
            q = rho & (LEFT - 1)
            k = LEFT - 1 - q if s == 2 else q
            targets.append(jnp.where(k < HALO, base + step_k * k + step_m * m, -1))
    return jnp.concatenate(targets, 0)


def prepare_kernel(
    owners, position, neighbour, code, own_hbm, taps_hbm, cot_hbm, wout_hbm, win_hbm,
    onehot, frame, conv, d_hidden, cot_ref, taps_ref, win_ref,
    own_ref, wout_ref, sems,
):
    copies = [
        pltpu.make_async_copy(src, dst, sems.at[n])
        for n, (src, dst) in enumerate(
            (
                (own_hbm, own_ref),
                (taps_hbm, taps_ref),
                (cot_hbm, cot_ref),
                (wout_hbm, wout_ref),
                (win_hbm, win_ref),
            )
        )
    ]
    for copy in copies:
        copy.start()
    target = side_targets(owners, neighbour, code, position[0])
    lane = lax.broadcasted_iota(jnp.int32, (SIDE_CELLS, 3 * N * N), 1)
    onehot[...] = jnp.where(target == lane, 1.0, 0.0).astype(BF16)
    corner = jnp.zeros((HALO, LEFT, LANES), F32)
    copies[0].wait()
    own = own_ref[...]
    rims = dot(onehot[:, : N * N], own, 1, 0)
    inner = own.astype(F32).reshape(N, N, C)
    for l in range(C // LANES):
        lanes = slice(l * LANES, (l + 1) * LANES)
        for top in (0, HALO + N):
            for left in (0, LEFT + N):
                frame[l, top : top + HALO, left : left + LEFT, :] = corner
        for rows, cols, cells in RIMS:
            frame[l, rows, cols, :] = rims[cells, lanes].reshape(span(rows), span(cols), LANES)
        frame[l, HALO : HALO + N, LEFT : LEFT + N, :] = inner[:, :, lanes]
    copies[1].wait()
    for l in range(C // LANES):
        lanes = slice(l * LANES, (l + 1) * LANES)
        acc = [None] * N
        for b in range(TAPS):
            off = tap_offset(b)
            coef = [taps_ref[a * TAPS + b : a * TAPS + b + 1, lanes] for a in range(TAPS)]
            for r in range(ROWS):
                x = frame[l, r, off : off + N, :]
                for a in range(TAPS):
                    i = r - STEP * a
                    if 0 <= i < N:
                        term = x * coef[a]
                        acc[i] = term if acc[i] is None else acc[i] + term
        for i in range(N):
            conv[i * N : (i + 1) * N, lanes] = acc[i]
    copies[2].wait()
    copies[3].wait()
    d_hidden[...] = dot(cot_ref[...], wout_ref[...], 1, 1)
    copies[4].wait()


def one_kernel(one_ref, onehot, rims):
    rims[...] = dot(onehot[:, N * N : 2 * N * N], one_ref[...], 1, 0)


def add_rims(rims_ref, two_ref, onehot, taps_ref, frame, conv, alone):
    rims = rims_ref[...] + dot(onehot[:, 2 * N * N :], two_ref[...], 1, 0)
    alone[...] = jnp.zeros(alone.shape, F32)
    for l in range(C // LANES):
        lanes = slice(l * LANES, (l + 1) * LANES)
        for rows, cols, cells in RIMS:
            block = rims[cells, lanes].reshape(span(rows), span(cols), LANES)
            frame[l, rows, cols, :] += block
            alone[l, rows, cols, :] = block
    for l in range(C // LANES):
        lanes = slice(l * LANES, (l + 1) * LANES)
        acc = [[conv[i * N + 8 * t : i * N + 8 * t + 8, lanes] for t in range(2)] for i in range(N)]
        for b in range(TAPS):
            off = tap_offset(b)
            coef = [taps_ref[a * TAPS + b : a * TAPS + b + 1, lanes] for a in range(TAPS)]
            for r in range(ROWS):
                middle = HALO <= r < HALO + N
                for t in range(2):
                    start = off + 8 * t
                    if middle and start >= LEFT and start + 8 <= LEFT + N:
                        continue
                    x = alone[l, r, start : start + 8, :]
                    for a in range(TAPS):
                        i = r - STEP * a
                        if 0 <= i < N:
                            acc[i][t] = acc[i][t] + x * coef[a]
        for i in range(N):
            for t in range(2):
                conv[i * N + 8 * t : i * N + 8 * t + 8, lanes] = acc[i][t]


def forward_kernel(
    core, frame_in, conv_in, rims_ref, two_ref, onehot, d_hidden_ref, cot_ref, taps_ref, win_ref,
    send_ref, keep_ref, dconv_ref, frame, conv, alone,
):
    del frame_in, conv_in
    add_rims(rims_ref, two_ref, onehot, taps_ref, frame, conv, alone)
    value = conv[...]
    centred = value - jnp.mean(value, -1, keepdims=True)
    inv_std = lax.rsqrt(jnp.mean(centred * centred, -1, keepdims=True) + 1e-06)
    normed_f = centred * inv_std
    normed = normed_f.astype(BF16)
    cot = cot_ref[...]
    first = core[0] == 0
    d_normed = None
    for h in range(GROUP):
        cols = slice(h * C, (h + 1) * C)
        w_in = win_ref[:, cols]
        pre = dot(normed, w_in, 1, 0)
        square = pre * pre
        t = jnp.tanh(pre * (GELU_A + (GELU_A * GELU_B) * square))
        half = 0.5 + 0.5 * t
        value = pre * half
        hidden = value.astype(BF16)
        slope = half + value * ((1.0 - t) * (GELU_A + (3.0 * GELU_A * GELU_B) * square))
        d_pre = (d_hidden_ref[:, cols] * slope).astype(BF16)
        part_out = dot(hidden, cot, 0, 0).astype(BF16)
        part_in = dot(normed, d_pre, 0, 0).astype(BF16)
        send_ref[h] = jnp.where(first, part_out, part_in)
        keep_ref[h] = jnp.where(first, part_in, part_out)
        back = dot(d_pre, w_in, 1, 1)
        d_normed = back if d_normed is None else d_normed + back
    dconv_ref[...] = inv_std * (
        d_normed
        - jnp.mean(d_normed, -1, keepdims=True)
        - normed_f * jnp.mean(d_normed * normed_f, -1, keepdims=True)
    )


def tap_sums(frame, dconv_ref, out_ref):
    out_ref[...] = jnp.zeros(out_ref.shape, F32)
    for l in range(C // LANES):
        lanes = slice(l * LANES, (l + 1) * LANES)
        grad = [dconv_ref[i * N : (i + 1) * N, lanes] for i in range(N)]
        for b in range(TAPS):
            off = tap_offset(b)
            acc = [None] * TAPS
            for r in range(ROWS):
                x = frame[l, r, off : off + N, :]
                for a in range(TAPS):
                    i = r - STEP * a
                    if 0 <= i < N:
                        term = x * grad[i]
                        acc[a] = term if acc[a] is None else acc[a] + term
            for a in range(TAPS):
                t = a * TAPS + b
                out_ref[t // EXTRA, t % EXTRA : t % EXTRA + 1, lanes] = jnp.sum(
                    acc[a], 0, keepdims=True
                )


def tap_kernel(frame, dconv_in, keep_in, sums_ref, dconv_ref, keep_ref):
    del dconv_in, keep_in, keep_ref
    tap_sums(frame, dconv_ref, sums_ref)


def backward_kernel(
    onehot, dconv_ref, taps_ref, cot_hbm, own_ref, one_ref, two_ref, shifted, rim, cot_ref, sem,
):
    copy = pltpu.make_async_copy(cot_hbm, cot_ref, sem)
    copy.start()
    residues = (2, 4, 6, 0)
    pad = jnp.zeros((ROWS, 8, LANES), F32)
    for l in range(C // LANES):
        lanes = slice(l * LANES, (l + 1) * LANES)
        grad = [
            [dconv_ref[i * N + 8 * t : i * N + 8 * t + 8, lanes] for t in range(2)]
            for i in range(N)
        ]
        for n, s in enumerate(residues):
            shifted[l, n, :, 0:8, :] = pad
            shifted[l, n, :, 32:40, :] = pad
            pieces = [(b, tap_offset(b) // 8) for b in range(TAPS) if tap_offset(b) % 8 == s]
            coef = {
                (a, b): taps_ref[a * TAPS + b : a * TAPS + b + 1, lanes]
                for a in range(TAPS)
                for b, _ in pieces
            }
            for r in range(ROWS):
                acc = [None] * 3
                for a in range(TAPS):
                    i = r - STEP * a
                    if 0 <= i < N:
                        for b, up in pieces:
                            for t in range(2):
                                term = grad[i][t] * coef[a, b]
                                acc[t + up] = term if acc[t + up] is None else acc[t + up] + term
                for t in range(3):
                    shifted[l, n, r, 8 + 8 * t : 16 + 8 * t, :] = (
                        jnp.zeros((8, LANES), F32) if acc[t] is None else acc[t]
                    )

        def gather(rows, first_col, count):
            total = None
            for n, s in enumerate(residues):
                at = 8 + first_col - s
                piece = shifted[l, n, rows, at : at + count, :]
                total = piece if total is None else total + piece
            return total

        top = gather(slice(0, HALO), LEFT, N)
        bottom = gather(slice(HALO + N, ROWS), LEFT, N)
        middle = slice(HALO, HALO + N)
        left = gather(middle, 0, 8)
        right = gather(middle, LEFT + N, 8)
        inner = gather(middle, LEFT, N)
        at = 0
        for block in (top, bottom, left, right):
            n = block.shape[0] * block.shape[1]
            rim[at : at + n, lanes] = block.reshape(n, LANES).astype(BF16)
            at += n
        own_ref[:, lanes] = inner.reshape(N * N, LANES)
    copy.wait()
    cells = rim[...]
    own_ref[...] += cot_ref[...].astype(F32) + dot(onehot[:, : N * N], cells, 0, 0)
    one_ref[...] = dot(onehot[:, N * N : 2 * N * N], cells, 0, 0).astype(BF16)
    two_ref[...] = dot(onehot[:, 2 * N * N :], cells, 0, 0).astype(BF16)


def spread_kernel(place, keep_ref, got_ref, taps_ref, own_ref, one_ref, two_ref, three_ref):
    for d, out in enumerate((own_ref, one_ref, two_ref, three_ref)):
        j = place[0] ^ d
        out[:C, :] = (keep_ref[j].astype(F32) + got_ref[j].astype(F32)).astype(out.dtype)
        out[C:, :] = taps_ref[j].astype(out.dtype)


def store_kernel(scale, picks, given, last, core, mine_at, theirs_at, *refs):
    count = len(picks) + (2 * GROUP if last else 0)
    blocks, taps = refs[: len(picks)], refs[len(picks) : count]
    refs = refs[count + given :]
    in_hbm, out_hbm = refs[:2]
    copies = []
    if last:
        kernel_hbm, stage, sems, rows, kernel_ref = refs[2:]
        for n, block in enumerate(taps):
            at = (mine_at if n < GROUP else theirs_at)[0] ^ (n % GROUP)
            rows[n // GROUP, at] = block[C:, :].astype(F32)
        for j in range(GROUP):
            n = min(EXTRA, TAPS * TAPS - j * EXTRA)
            kernel_ref[j * EXTRA : j * EXTRA + n, :] = (rows[0, j, :n, :] + rows[1, j, :n, :]) * scale
        copies.append(pltpu.make_async_copy(kernel_ref, kernel_hbm, sems.at[GROUP]))
        copies[0].start()
    else:
        stage, sems = refs[2:]
    first = core[0] == 0
    pairs = []
    for n, (half, d) in enumerate(picks):
        stage[n] = blocks[n][:C, :].astype(F32) * scale
        at = pl.ds(pl.multiple_of(((theirs_at if half else mine_at)[0] ^ d) * C, C), C)
        into_in = pltpu.make_async_copy(stage.at[n], in_hbm.at[:, at], sems.at[n])
        into_out = pltpu.make_async_copy(stage.at[n], out_hbm.at[at, :], sems.at[n])
        to_in = jnp.logical_not(first) if half else first
        pl.when(to_in)(into_in.start)
        pl.when(jnp.logical_not(to_in))(into_out.start)
        pairs.append((to_in, into_in, into_out))
    for copy in copies:
        copy.wait()
    for to_in, into_in, into_out in pairs:
        pl.when(to_in)(into_in.wait)
        pl.when(jnp.logical_not(to_in))(into_out.wait)


def join_kernel(own_ref, other_ref, out_ref):
    out_ref[...] = (own_ref[...] + other_ref[...].astype(F32)).astype(out_ref.dtype)


def in_hbm(x):
    return pltpu.with_memory_space_constraint(x, pltpu.HBM)


def in_vmem(x):
    return pltpu.with_memory_space_constraint(x, pltpu.VMEM)


def call(kernel, outs, scratch=(), specs=(), flops=300_000_000, aliases={}, out_specs=None, vmem=16):
    return pl.pallas_call(
        kernel,
        out_shape=outs,
        in_specs=specs,
        out_specs=out_specs or jax.tree.map(lambda _: VMEM, outs),
        scratch_shapes=scratch,
        input_output_aliases=aliases,
        compiler_params=pltpu.CompilerParams(vmem_limit_bytes=vmem * 1024 * 1024),
        cost_estimate=pl.CostEstimate(flops=flops, bytes_accessed=4_000_000, transcendentals=0),
    )


def body(features, cotangent, kernel, weight_in, weight_out, tile_neighbour, edge_code):
    owners = lax.axis_size("tile")
    members = lax.axis_size("ens")
    position = lax.axis_index("tile")
    member = lax.axis_index("ens")
    devices = owners * members
    scale = 1.0 / math.sqrt(devices * N * N)
    both = ("tile", "ens")
    struct = jax.ShapeDtypeStruct

    def one_over(x):
        return lax.ppermute(x, "tile", [(i, i ^ 1) for i in range(owners)])

    def two_over(x):
        moves = [(i, (i + 1 if i % 2 else i - 1) % owners) for i in range(owners)]
        return lax.ppermute(x, "tile", moves)

    index = position * members + member
    free = [1 << n for n in range(2, members.bit_length() - 1)]
    free += [members << n for n in range(1, owners.bit_length() - 1)]
    pairs = ((2, members), (free[0], free[1]))
    later = [tuple(free[n : n + 2]) for n in range(2, len(free), 2)]

    def swap(x, even, odd):
        return lax.ppermute(x, both, [(i, i ^ (odd if i % 2 else even)) for i in range(devices)])

    def digit(pair):
        return jnp.where(index & pair[0], 1, 0) + jnp.where(index & pair[1], 2, 0)

    core = member % 2
    digits = (digit(pairs[0]), digit(pairs[1]))
    mine_at = jnp.where(core == 0, digits[0], digits[1]).astype(jnp.int32).reshape(1)
    theirs_at = jnp.where(core == 0, digits[1], digits[0]).astype(jnp.int32).reshape(1)
    core = core.reshape(1).astype(jnp.int32)
    combos = [[p[0], p[1], p[0] + p[1]] for p in pairs]

    own = features.reshape(N * N, C)
    cot_rows = cotangent.reshape(N * N, C)
    one = one_over(own)
    two = two_over(own)

    frame = pltpu.VMEM((2, ROWS, FRAME, LANES), F32)
    cells = pltpu.VMEM((N * N, C), F32)
    onehot, frame_own, conv_own, d_hidden, cot, taps, w_in = call(
        functools.partial(prepare_kernel, owners),
        (
            pltpu.VMEM((SIDE_CELLS, 3 * N * N), BF16),
            frame,
            cells,
            pltpu.VMEM((N * N, HID), F32),
            pltpu.VMEM((N * N, C), BF16),
            pltpu.VMEM((TAPS * TAPS, C), F32),
            pltpu.VMEM((C, HID), BF16),
        ),
        [
            pltpu.VMEM((N * N, C), BF16),
            pltpu.VMEM((HID, C), BF16),
            pltpu.SemaphoreType.DMA((5,)),
        ],
        [SMEM] * 3 + [HBM] * 5,
    )(
        position.reshape(1).astype(jnp.int32),
        tile_neighbour,
        edge_code,
        *map(in_hbm, (own, kernel, cot_rows, weight_out, weight_in)),
    )
    rims = call(one_kernel, pltpu.VMEM((SIDE_CELLS, C), F32), (), [VMEM] * 2)(one, onehot)
    half = pltpu.VMEM((GROUP, C, C), BF16)
    send, keep, dconv, frame_two, _ = call(
        forward_kernel,
        (half, half, cells, frame, cells),
        [frame],
        [SMEM] + [VMEM] * 9,
        flops=1_000_000_000,
        aliases={1: 3, 2: 4},
    )(core, frame_own, conv_own, rims, two, onehot, d_hidden, cot, taps, w_in)
    got = swap(send, 1, 1)
    part_taps, dconv, keep = call(
        tap_kernel,
        (pltpu.VMEM((GROUP, EXTRA, C), F32), cells, half),
        (),
        [VMEM] * 3,
        aliases={1: 1, 2: 2},
    )(frame_two, dconv, keep)
    block = pltpu.VMEM((C + EXTRA, C), BF16)
    pieces = call(
        spread_kernel, (block,) * GROUP, (), [SMEM] + [VMEM] * 3
    )(mine_at, keep, in_vmem(got), part_taps)
    total = pieces[0].astype(F32)
    for d in STARTS[0]:
        total = total + swap(pieces[d], combos[0][d - 1], combos[1][d - 1]).astype(F32)
    total = total.astype(BF16)

    grad_own, grad_one, grad_two = call(
        backward_kernel,
        (cells, pltpu.VMEM((N * N, C), BF16), pltpu.VMEM((N * N, C), BF16)),
        [
            pltpu.VMEM((2, 4, ROWS, 40, LANES), F32),
            pltpu.VMEM((SIDE_CELLS, C), BF16),
            pltpu.VMEM((N * N, C), BF16),
            pltpu.SemaphoreType.DMA,
        ],
        [VMEM] * 3 + [HBM],
    )(onehot, dconv, taps, in_hbm(cot_rows))
    back_two = two_over(grad_two)
    back_one = one_over(grad_one)
    for even, odd in [(pairs[1], pairs[0])] + [(p, p) for p in later]:
        if len(even) == 2:
            even, odd = (*even, sum(even)), (*odd, sum(odd))
        order = [d for d in reversed(STARTS[1]) if d <= len(even)]
        got = {d: swap(total, even[d - 1], odd[d - 1]).astype(F32) for d in order}
        summed = total.astype(F32) + got[1]
        if len(even) == 3:
            summed = summed + (got[2] + got[3])
        total = summed.astype(BF16)
    joined = call(
        join_kernel, pltpu.VMEM((N * N, C), F32), (), [VMEM] * 2, flops=JOIN_COST
    )(grad_own, back_one)
    total, joined = lax.optimization_barrier((total, joined))
    mine = {d: swap(total, combos[0][d - 1], combos[1][d - 1]) for d in reversed(STARTS[2])}
    mine = [total, mine[1], mine[2], mine[3]]
    grad_features = call(
        join_kernel, struct((N * N, C), BF16), (), [VMEM] * 2, flops=JOIN_COST
    )(joined, back_two)
    mine[0], grad_features = lax.optimization_barrier((mine[0], grad_features))
    theirs = [swap(x, 1, 1) for x in mine]
    grads = (struct((C, HID), F32), struct((HID, C), F32))
    stage = [pltpu.VMEM((GROUP, C, C), F32), pltpu.SemaphoreType.DMA((GROUP + 1,))]
    halves = (mine, theirs)

    def store(picks, given, last=False):
        blocks = [halves[half][d] for half, d in picks] + ([*mine, *theirs] if last else [])
        count = 3 + len(blocks)
        return call(
            functools.partial(store_kernel, scale, picks, len(given), last),
            (*grads, struct((TAPS * TAPS, C), F32)) if last else grads,
            stage
            + (
                [pltpu.VMEM((2, GROUP, EXTRA, C), F32), pltpu.VMEM((TAPS * TAPS, C), F32)]
                if last
                else []
            ),
            [SMEM] * 3 + [VMEM] * len(blocks) + [ANY] * len(given),
            out_specs=(ANY,) * (3 if last else 2),
            aliases={count + n: n for n in range(len(given))},
        )(core, mine_at, theirs_at, *blocks, *given)

    given = store([(0, d) for d in range(GROUP)], ())
    grad_in, grad_out, grad_kernel = store([(1, d) for d in range(GROUP)], given, True)
    return grad_features.reshape(features.shape), grad_kernel, grad_in, grad_out


def solution(mesh):
    halved = P("ens", "tile", None, None, None)
    in_specs = (halved, halved, P(), P(), P(), P("tile", None), P("tile", None))
    out_specs = (halved, P(), P(), P())
    return jax.shard_map(body, mesh=mesh, in_specs=in_specs, out_specs=out_specs, check_vma=False)
```

```python
import functools
import math

import jax
import jax.numpy as jnp
from jax import lax
from jax.experimental import pallas as pl
from jax.experimental.pallas import tpu as pltpu
from jax.sharding import PartitionSpec as P

C = 256
HID = 1024
TAPS = 7
STEP = 2
HALO = 6
N = 16
ROWS = N + 2 * HALO
LANES = 128
FRAME = 32
LEFT = 8
GROUP = 4
STARTS = ((3, 2, 1), (3, 2, 1), (3, 2, 1))
JOIN_COST = 30_000_000_000
EXTRA = 16
F32 = jnp.float32
BF16 = jnp.bfloat16
GELU_A = math.sqrt(2.0 / math.pi)
GELU_B = 0.044715
SIDE_CELLS = 2 * HALO * N + 2 * LEFT * N
RIMS = (
    (slice(0, HALO), slice(LEFT, LEFT + N), slice(0, 96)),
    (slice(HALO + N, ROWS), slice(LEFT, LEFT + N), slice(96, 192)),
    (slice(HALO, HALO + N), slice(0, LEFT), slice(192, 320)),
    (slice(HALO, HALO + N), slice(LEFT + N, FRAME), slice(320, 448)),
)
VMEM = pl.BlockSpec(memory_space=pltpu.VMEM)
ANY = pl.BlockSpec(memory_space=pl.ANY)
HBM = pl.BlockSpec(memory_space=pltpu.HBM)
SMEM = pl.BlockSpec(memory_space=pltpu.SMEM)


def span(s):
    return s.stop - s.start


def dot(a, b, ca, cb):
    return lax.dot_general(a, b, (((ca,), (cb,)), ((), ())), preferred_element_type=F32)


def tap_offset(b):
    return LEFT - HALO + STEP * b


def span(s):
    return s.stop - s.start


def side_targets(owners, neighbour, code, position):
    targets = []
    for s in range(4):
        offset = lax.rem(neighbour[0, s] - position + 1 + owners, owners)
        first = (offset == 0) == (lax.rem(position, 2) == 1)
        source = jnp.where(offset == 1, 0, jnp.where(first, 1, 2))
        edge = code[0, s] & 3
        flipped = (code[0, s] >> 2) & 1
        along = jnp.where(edge < 2, 1, N)
        across = jnp.where(edge < 2, N, 1)
        far = edge & 1
        base = source * (N * N) + flipped * (N - 1) * along + far * (N - 1) * across
        step_k = across * (1 - 2 * far)
        step_m = along * (1 - 2 * flipped)
        n = HALO * N if s < 2 else LEFT * N
        rho = lax.broadcasted_iota(jnp.int32, (n, 1), 0)
        if s < 2:
            m = rho & (N - 1)
            k = rho >> 4
            if s == 0:
                k = HALO - 1 - k
            targets.append(base + step_k * k + step_m * m)
        else:
            m = rho >> 3
            q = rho & (LEFT - 1)
            k = LEFT - 1 - q if s == 2 else q
            targets.append(jnp.where(k < HALO, base + step_k * k + step_m * m, -1))
    return jnp.concatenate(targets, 0)


def prepare_kernel(
    owners, position, neighbour, code, own_hbm, taps_hbm, cot_hbm, wout_hbm, win_hbm,
    onehot, frame, conv, d_hidden, cot_ref, taps_ref, win_ref,
    own_ref, wout_ref, sems,
):
    copies = [
        pltpu.make_async_copy(src, dst, sems.at[n])
        for n, (src, dst) in enumerate(
            (
                (own_hbm, own_ref),
                (taps_hbm, taps_ref),
                (cot_hbm, cot_ref),
                (wout_hbm, wout_ref),
                (win_hbm, win_ref),
            )
        )
    ]
    for copy in copies:
        copy.start()
    target = side_targets(owners, neighbour, code, position[0])
    lane = lax.broadcasted_iota(jnp.int32, (SIDE_CELLS, 3 * N * N), 1)
    onehot[...] = jnp.where(target == lane, 1.0, 0.0).astype(BF16)
    corner = jnp.zeros((HALO, LEFT, LANES), F32)
    copies[0].wait()
    own = own_ref[...]
    rims = dot(onehot[:, : N * N], own, 1, 0)
    inner = own.astype(F32).reshape(N, N, C)
    for l in range(C // LANES):
        lanes = slice(l * LANES, (l + 1) * LANES)
        for top in (0, HALO + N):
            for left in (0, LEFT + N):
                frame[l, top : top + HALO, left : left + LEFT, :] = corner
        for rows, cols, cells in RIMS:
            frame[l, rows, cols, :] = rims[cells, lanes].reshape(span(rows), span(cols), LANES)
        frame[l, HALO : HALO + N, LEFT : LEFT + N, :] = inner[:, :, lanes]
    copies[1].wait()
    for l in range(C // LANES):
        lanes = slice(l * LANES, (l + 1) * LANES)
        acc = [None] * N
        for b in range(TAPS):
            off = tap_offset(b)
            coef = [taps_ref[a * TAPS + b : a * TAPS + b + 1, lanes] for a in range(TAPS)]
            for r in range(ROWS):
                x = frame[l, r, off : off + N, :]
                for a in range(TAPS):
                    i = r - STEP * a
                    if 0 <= i < N:
                        term = x * coef[a]
                        acc[i] = term if acc[i] is None else acc[i] + term
        for i in range(N):
            conv[i * N : (i + 1) * N, lanes] = acc[i]
    copies[2].wait()
    copies[3].wait()
    d_hidden[...] = dot(cot_ref[...], wout_ref[...], 1, 1)
    copies[4].wait()


def one_kernel(one_ref, onehot, rims):
    rims[...] = dot(onehot[:, N * N : 2 * N * N], one_ref[...], 1, 0)


def add_rims(rims_ref, two_ref, onehot, taps_ref, frame, conv, alone):
    rims = rims_ref[...] + dot(onehot[:, 2 * N * N :], two_ref[...], 1, 0)
    alone[...] = jnp.zeros(alone.shape, F32)
    for l in range(C // LANES):
        lanes = slice(l * LANES, (l + 1) * LANES)
        for rows, cols, cells in RIMS:
            block = rims[cells, lanes].reshape(span(rows), span(cols), LANES)
            frame[l, rows, cols, :] += block
            alone[l, rows, cols, :] = block
    for l in range(C // LANES):
        lanes = slice(l * LANES, (l + 1) * LANES)
        acc = [[conv[i * N + 8 * t : i * N + 8 * t + 8, lanes] for t in range(2)] for i in range(N)]
        for b in range(TAPS):
            off = tap_offset(b)
            coef = [taps_ref[a * TAPS + b : a * TAPS + b + 1, lanes] for a in range(TAPS)]
            for r in range(ROWS):
                middle = HALO <= r < HALO + N
                for t in range(2):
                    start = off + 8 * t
                    if middle and start >= LEFT and start + 8 <= LEFT + N:
                        continue
                    x = alone[l, r, start : start + 8, :]
                    for a in range(TAPS):
                        i = r - STEP * a
                        if 0 <= i < N:
                            acc[i][t] = acc[i][t] + x * coef[a]
        for i in range(N):
            for t in range(2):
                conv[i * N + 8 * t : i * N + 8 * t + 8, lanes] = acc[i][t]


def forward_kernel(
    core, frame_in, conv_in, rims_ref, two_ref, onehot, d_hidden_ref, cot_ref, taps_ref, win_ref,
    send_ref, keep_ref, dconv_ref, frame, conv, alone,
):
    del frame_in, conv_in
    add_rims(rims_ref, two_ref, onehot, taps_ref, frame, conv, alone)
    value = conv[...]
    centred = value - jnp.mean(value, -1, keepdims=True)
    inv_std = lax.rsqrt(jnp.mean(centred * centred, -1, keepdims=True) + 1e-06)
    normed_f = centred * inv_std
    normed = normed_f.astype(BF16)
    cot = cot_ref[...]
    first = core[0] == 0
    d_normed = None
    for h in range(GROUP):
        cols = slice(h * C, (h + 1) * C)
        w_in = win_ref[:, cols]
        pre = dot(normed, w_in, 1, 0)
        square = pre * pre
        t = jnp.tanh(pre * (GELU_A + (GELU_A * GELU_B) * square))
        half = 0.5 + 0.5 * t
        value = pre * half
        hidden = value.astype(BF16)
        slope = half + value * ((1.0 - t) * (GELU_A + (3.0 * GELU_A * GELU_B) * square))
        d_pre = (d_hidden_ref[:, cols] * slope).astype(BF16)
        part_out = dot(hidden, cot, 0, 0).astype(BF16)
        part_in = dot(normed, d_pre, 0, 0).astype(BF16)
        send_ref[h] = jnp.where(first, part_out, part_in)
        keep_ref[h] = jnp.where(first, part_in, part_out)
        back = dot(d_pre, w_in, 1, 1)
        d_normed = back if d_normed is None else d_normed + back
    dconv_ref[...] = inv_std * (
        d_normed
        - jnp.mean(d_normed, -1, keepdims=True)
        - normed_f * jnp.mean(d_normed * normed_f, -1, keepdims=True)
    )


def tap_sums(frame, dconv_ref, out_ref):
    out_ref[...] = jnp.zeros(out_ref.shape, F32)
    for l in range(C // LANES):
        lanes = slice(l * LANES, (l + 1) * LANES)
        grad = [dconv_ref[i * N : (i + 1) * N, lanes] for i in range(N)]
        for b in range(TAPS):
            off = tap_offset(b)
            acc = [None] * TAPS
            for r in range(ROWS):
                x = frame[l, r, off : off + N, :]
                for a in range(TAPS):
                    i = r - STEP * a
                    if 0 <= i < N:
                        term = x * grad[i]
                        acc[a] = term if acc[a] is None else acc[a] + term
            for a in range(TAPS):
                t = a * TAPS + b
                out_ref[t // EXTRA, t % EXTRA : t % EXTRA + 1, lanes] = jnp.sum(
                    acc[a], 0, keepdims=True
                )


def tap_kernel(frame, dconv_in, keep_in, sums_ref, dconv_ref, keep_ref):
    del dconv_in, keep_in, keep_ref
    tap_sums(frame, dconv_ref, sums_ref)


def backward_kernel(
    onehot, dconv_ref, taps_ref, cot_hbm, own_ref, one_ref, two_ref, shifted, rim, cot_ref, sem,
):
    copy = pltpu.make_async_copy(cot_hbm, cot_ref, sem)
    copy.start()
    residues = (2, 4, 6, 0)
    pad = jnp.zeros((ROWS, 8, LANES), F32)
    for l in range(C // LANES):
        lanes = slice(l * LANES, (l + 1) * LANES)
        grad = [
            [dconv_ref[i * N + 8 * t : i * N + 8 * t + 8, lanes] for t in range(2)]
            for i in range(N)
        ]
        for n, s in enumerate(residues):
            shifted[l, n, :, 0:8, :] = pad
            shifted[l, n, :, 32:40, :] = pad
            pieces = [(b, tap_offset(b) // 8) for b in range(TAPS) if tap_offset(b) % 8 == s]
            coef = {
                (a, b): taps_ref[a * TAPS + b : a * TAPS + b + 1, lanes]
                for a in range(TAPS)
                for b, _ in pieces
            }
            for r in range(ROWS):
                acc = [None] * 3
                for a in range(TAPS):
                    i = r - STEP * a
                    if 0 <= i < N:
                        for b, up in pieces:
                            for t in range(2):
                                term = grad[i][t] * coef[a, b]
                                acc[t + up] = term if acc[t + up] is None else acc[t + up] + term
                for t in range(3):
                    shifted[l, n, r, 8 + 8 * t : 16 + 8 * t, :] = (
                        jnp.zeros((8, LANES), F32) if acc[t] is None else acc[t]
                    )

        def gather(rows, first_col, count):
            total = None
            for n, s in enumerate(residues):
                at = 8 + first_col - s
                piece = shifted[l, n, rows, at : at + count, :]
                total = piece if total is None else total + piece
            return total

        top = gather(slice(0, HALO), LEFT, N)
        bottom = gather(slice(HALO + N, ROWS), LEFT, N)
        middle = slice(HALO, HALO + N)
        left = gather(middle, 0, 8)
        right = gather(middle, LEFT + N, 8)
        inner = gather(middle, LEFT, N)
        at = 0
        for block in (top, bottom, left, right):
            n = block.shape[0] * block.shape[1]
            rim[at : at + n, lanes] = block.reshape(n, LANES).astype(BF16)
            at += n
        own_ref[:, lanes] = inner.reshape(N * N, LANES)
    copy.wait()
    cells = rim[...]
    own_ref[...] += cot_ref[...].astype(F32) + dot(onehot[:, : N * N], cells, 0, 0)
    one_ref[...] = dot(onehot[:, N * N : 2 * N * N], cells, 0, 0).astype(BF16)
    two_ref[...] = dot(onehot[:, 2 * N * N :], cells, 0, 0).astype(BF16)


def spread_kernel(place, keep_ref, got_ref, taps_ref, own_ref, one_ref, two_ref, three_ref):
    for d, out in enumerate((own_ref, one_ref, two_ref, three_ref)):
        j = place[0] ^ d
        out[:C, :] = (keep_ref[j].astype(F32) + got_ref[j].astype(F32)).astype(out.dtype)
        out[C:, :] = taps_ref[j].astype(out.dtype)


def store_kernel(scale, picks, given, last, core, mine_at, theirs_at, *refs):
    count = len(picks) + (2 * GROUP if last else 0)
    blocks, taps = refs[: len(picks)], refs[len(picks) : count]
    refs = refs[count + given :]
    in_hbm, out_hbm = refs[:2]
    copies = []
    if last:
        kernel_hbm, stage, sems, rows, kernel_ref = refs[2:]
        for n, block in enumerate(taps):
            at = (mine_at if n < GROUP else theirs_at)[0] ^ (n % GROUP)
            rows[n // GROUP, at] = block[C:, :].astype(F32)
        for j in range(GROUP):
            n = min(EXTRA, TAPS * TAPS - j * EXTRA)
            kernel_ref[j * EXTRA : j * EXTRA + n, :] = (rows[0, j, :n, :] + rows[1, j, :n, :]) * scale
        copies.append(pltpu.make_async_copy(kernel_ref, kernel_hbm, sems.at[GROUP]))
        copies[0].start()
    else:
        stage, sems = refs[2:]
    first = core[0] == 0
    pairs = []
    for n, (half, d) in enumerate(picks):
        stage[n] = blocks[n][:C, :].astype(F32) * scale
        at = pl.ds(pl.multiple_of(((theirs_at if half else mine_at)[0] ^ d) * C, C), C)
        into_in = pltpu.make_async_copy(stage.at[n], in_hbm.at[:, at], sems.at[n])
        into_out = pltpu.make_async_copy(stage.at[n], out_hbm.at[at, :], sems.at[n])
        to_in = jnp.logical_not(first) if half else first
        pl.when(to_in)(into_in.start)
        pl.when(jnp.logical_not(to_in))(into_out.start)
        pairs.append((to_in, into_in, into_out))
    for copy in copies:
        copy.wait()
    for to_in, into_in, into_out in pairs:
        pl.when(to_in)(into_in.wait)
        pl.when(jnp.logical_not(to_in))(into_out.wait)


def join_kernel(own_ref, one_ref, two_ref, out_ref):
    out_ref[...] = (own_ref[...] + one_ref[...].astype(F32) + two_ref[...].astype(F32)).astype(BF16)


def in_hbm(x):
    return pltpu.with_memory_space_constraint(x, pltpu.HBM)


def in_vmem(x):
    return pltpu.with_memory_space_constraint(x, pltpu.VMEM)


def call(kernel, outs, scratch=(), specs=(), flops=300_000_000, aliases={}, out_specs=None, vmem=16):
    return pl.pallas_call(
        kernel,
        out_shape=outs,
        in_specs=specs,
        out_specs=out_specs or jax.tree.map(lambda _: VMEM, outs),
        scratch_shapes=scratch,
        input_output_aliases=aliases,
        compiler_params=pltpu.CompilerParams(vmem_limit_bytes=vmem * 1024 * 1024),
        cost_estimate=pl.CostEstimate(flops=flops, bytes_accessed=4_000_000, transcendentals=0),
    )


def body(features, cotangent, kernel, weight_in, weight_out, tile_neighbour, edge_code):
    owners = lax.axis_size("tile")
    members = lax.axis_size("ens")
    position = lax.axis_index("tile")
    member = lax.axis_index("ens")
    devices = owners * members
    scale = 1.0 / math.sqrt(devices * N * N)
    both = ("tile", "ens")
    struct = jax.ShapeDtypeStruct

    def one_over(x):
        return lax.ppermute(x, "tile", [(i, i ^ 1) for i in range(owners)])

    def two_over(x):
        moves = [(i, (i + 1 if i % 2 else i - 1) % owners) for i in range(owners)]
        return lax.ppermute(x, "tile", moves)

    index = position * members + member
    free = [1 << n for n in range(2, members.bit_length() - 1)]
    free += [members << n for n in range(1, owners.bit_length() - 1)]
    pairs = ((2, members), (free[0], free[1]))
    later = [tuple(free[n : n + 2]) for n in range(2, len(free), 2)]

    def swap(x, even, odd):
        return lax.ppermute(x, both, [(i, i ^ (odd if i % 2 else even)) for i in range(devices)])

    def digit(pair):
        return jnp.where(index & pair[0], 1, 0) + jnp.where(index & pair[1], 2, 0)

    core = member % 2
    digits = (digit(pairs[0]), digit(pairs[1]))
    mine_at = jnp.where(core == 0, digits[0], digits[1]).astype(jnp.int32).reshape(1)
    theirs_at = jnp.where(core == 0, digits[1], digits[0]).astype(jnp.int32).reshape(1)
    core = core.reshape(1).astype(jnp.int32)
    combos = [[p[0], p[1], p[0] + p[1]] for p in pairs]

    own = features.reshape(N * N, C)
    cot_rows = cotangent.reshape(N * N, C)
    one = one_over(own)
    two = two_over(own)

    frame = pltpu.VMEM((2, ROWS, FRAME, LANES), F32)
    cells = pltpu.VMEM((N * N, C), F32)
    onehot, frame_own, conv_own, d_hidden, cot, taps, w_in = call(
        functools.partial(prepare_kernel, owners),
        (
            pltpu.VMEM((SIDE_CELLS, 3 * N * N), BF16),
            frame,
            cells,
            pltpu.VMEM((N * N, HID), F32),
            pltpu.VMEM((N * N, C), BF16),
            pltpu.VMEM((TAPS * TAPS, C), F32),
            pltpu.VMEM((C, HID), BF16),
        ),
        [
            pltpu.VMEM((N * N, C), BF16),
            pltpu.VMEM((HID, C), BF16),
            pltpu.SemaphoreType.DMA((5,)),
        ],
        [SMEM] * 3 + [HBM] * 5,
    )(
        position.reshape(1).astype(jnp.int32),
        tile_neighbour,
        edge_code,
        *map(in_hbm, (own, kernel, cot_rows, weight_out, weight_in)),
    )
    rims = call(one_kernel, pltpu.VMEM((SIDE_CELLS, C), F32), (), [VMEM] * 2)(one, onehot)
    half = pltpu.VMEM((GROUP, C, C), BF16)
    send, keep, dconv, frame_two, _ = call(
        forward_kernel,
        (half, half, cells, frame, cells),
        [frame],
        [SMEM] + [VMEM] * 9,
        flops=1_000_000_000,
        aliases={1: 3, 2: 4},
    )(core, frame_own, conv_own, rims, two, onehot, d_hidden, cot, taps, w_in)
    got = swap(send, 1, 1)
    part_taps, dconv, keep = call(
        tap_kernel,
        (pltpu.VMEM((GROUP, EXTRA, C), F32), cells, half),
        (),
        [VMEM] * 3,
        aliases={1: 1, 2: 2},
    )(frame_two, dconv, keep)
    block = pltpu.VMEM((C + EXTRA, C), BF16)
    pieces = call(
        spread_kernel, (block,) * GROUP, (), [SMEM] + [VMEM] * 3
    )(mine_at, keep, in_vmem(got), part_taps)
    total = pieces[0].astype(F32)
    for d in STARTS[0]:
        total = total + swap(pieces[d], combos[0][d - 1], combos[1][d - 1]).astype(F32)
    total = total.astype(BF16)

    grad_own, grad_one, grad_two = call(
        backward_kernel,
        (cells, pltpu.VMEM((N * N, C), BF16), pltpu.VMEM((N * N, C), BF16)),
        [
            pltpu.VMEM((2, 4, ROWS, 40, LANES), F32),
            pltpu.VMEM((SIDE_CELLS, C), BF16),
            pltpu.VMEM((N * N, C), BF16),
            pltpu.SemaphoreType.DMA,
        ],
        [VMEM] * 3 + [HBM],
    )(onehot, dconv, taps, in_hbm(cot_rows))
    back_two = two_over(grad_two)
    back_one = one_over(grad_one)
    for even, odd in [(pairs[1], pairs[0])] + [(p, p) for p in later]:
        if len(even) == 2:
            even, odd = (*even, sum(even)), (*odd, sum(odd))
        order = [d for d in reversed(STARTS[1]) if d <= len(even)]
        got = {d: swap(total, even[d - 1], odd[d - 1]).astype(F32) for d in order}
        summed = total.astype(F32) + got[1]
        if len(even) == 3:
            summed = summed + (got[2] + got[3])
        total = summed.astype(BF16)
    mine = {d: swap(total, combos[0][d - 1], combos[1][d - 1]) for d in reversed(STARTS[2])}
    mine = [total, mine[1], mine[2], mine[3]]
    grad_features = call(
        join_kernel, struct((N * N, C), BF16), (), [VMEM] * 3, flops=JOIN_COST
    )(grad_own, back_one, back_two)
    mine[0], grad_features = lax.optimization_barrier((mine[0], grad_features))
    theirs = [swap(x, 1, 1) for x in mine]
    grads = (struct((C, HID), F32), struct((HID, C), F32))
    stage = [pltpu.VMEM((GROUP, C, C), F32), pltpu.SemaphoreType.DMA((GROUP + 1,))]
    halves = (mine, theirs)

    def store(picks, given, last=False):
        blocks = [halves[half][d] for half, d in picks] + ([*mine, *theirs] if last else [])
        count = 3 + len(blocks)
        return call(
            functools.partial(store_kernel, scale, picks, len(given), last),
            (*grads, struct((TAPS * TAPS, C), F32)) if last else grads,
            stage
            + (
                [pltpu.VMEM((2, GROUP, EXTRA, C), F32), pltpu.VMEM((TAPS * TAPS, C), F32)]
                if last
                else []
            ),
            [SMEM] * 3 + [VMEM] * len(blocks) + [ANY] * len(given),
            out_specs=(ANY,) * (3 if last else 2),
            aliases={count + n: n for n in range(len(given))},
        )(core, mine_at, theirs_at, *blocks, *given)

    given = store([(0, d) for d in range(GROUP)], ())
    grad_in, grad_out, grad_kernel = store([(1, d) for d in range(GROUP)], given, True)
    return grad_features.reshape(features.shape), grad_kernel, grad_in, grad_out


def solution(mesh):
    halved = P("ens", "tile", None, None, None)
    in_specs = (halved, halved, P(), P(), P(), P("tile", None), P("tile", None))
    out_specs = (halved, P(), P(), P())
    return jax.shard_map(body, mesh=mesh, in_specs=in_specs, out_specs=out_specs, check_vma=False)
```
